256 devices in a mesh: ctx: 16 (over z, core), exp: 16 (over x, y).
Axes of the slice: x: 4, y: 4, z: 8, core: 2. Of those that a mesh axis runs over, the one named last changes fastest.
Arguments:
- queries: bfloat16 [2048, 4096], P('exp'), may hold values from -16 to 16
- cache_kv: bfloat16 [2, 64, 4096, 512], P(None, 'exp', 'ctx'), may hold values from -16 to 16
- block_kv: bfloat16 [2, 64, 32, 512], P(None, 'exp', 'ctx'), may hold values from -6 to 6
- stream_in: bfloat16 [2048, 4096], P('exp'), may hold values from -6 to 6
- out_proj: bfloat16 [4096, 4096], P('ctx'), may hold values from -0.25 to 0.25
- norm_gain: float32 [4096], replicated, may hold values from 0.1 to 1.9
- expert_ids: int32 [2048, 8], P('exp'), may hold values from 0 to 127, all different within a row; in each aligned block of 128 rows (0 to 127, 128 to 255, ...) at most 16 rows name the same one
- gate_weights: float32 [2048, 8], P('exp'), may hold values from 0.03 to 0.3
- expert_in: bfloat16 [2, 16, 4096, 4096], P(None, 'exp', None, 'ctx'), may hold values from -0.09375 to 0.09375
- expert_out: bfloat16 [16, 4096, 4096], P('exp', 'ctx'), may hold values from -0.375 to 0.375
Outputs:
- mixed_out: bfloat16 [2048, 4096], P('exp', 'ctx')
The draws below stay inside these ranges and needn't reach their ends.
Inputs may be any that keep to these rules, and one draw needn't show every extreme that they name: `expert_ids`: each row names 8 different experts; in each aligned block of 128 rows (the rows of one index of exp) no expert is named by more than 16 rows, a bound that some block reaches.
All inputs are finite; a program needn't handle non-finite values.
Results may differ from the reference program's by a relative error of at most 0.035.
Values may be sent and summed in bfloat16 or wider, within the bound.
A program may use at most 192 MiB of HBM per device.

```python
import math
import jax
import jax.numpy as jnp
import numpy as np
from jax import lax

D = 4096
H = 32
KVH = 4
HD = 128
TOP = 8
EW = 512
MASKED = 32
OWNED = 8
EXPERTS = 128
SEQS_ALL = 64
ROWS_G = 128
ROWS = 2048
PROMPT = 4096
CAP = 16
N_EXP = 16


def draw_queries(key, part):
    key = jax.random.fold_in(key, 11)
    return jnp.clip(2.0 * jax.random.normal(key, (ROWS, H * HD), jnp.float32), -8.0, 8.0).astype(jnp.bfloat16)


def draw_cache_kv(key, part):
    key = jax.random.fold_in(key, 12)
    return jnp.clip(jax.random.normal(key, (2, SEQS_ALL, PROMPT, KVH * HD), jnp.float32), -4.0, 4.0).astype(jnp.bfloat16)


def draw_stream_in(key, part):
    key = jax.random.fold_in(key, 13)
    key_rows, key_base = jax.random.split(key, 2)
    row_scale = 10.0 ** jax.random.uniform(key_rows, (ROWS, 1), jnp.float32, -1.5, -0.5)
    col_scale = 10.0 ** (jnp.arange(D, dtype=jnp.float32) / D - 0.5)
    base_draw = jax.random.normal(key_base, (ROWS, D), jnp.float32)
    return jnp.clip(base_draw * row_scale * col_scale[None, :], -6.0, 6.0).astype(jnp.bfloat16)


def raised(entries, rng, source, target, blocks, factor):
    def block_of(axis_at):
        return (jnp.arange(entries.shape[axis_at]) // (entries.shape[axis_at] // blocks)).reshape((-1,) + (1,) * (entries.ndim - 1 - axis_at))

    first = jax.random.permutation(rng, blocks)[block_of(target)]
    other_side = (block_of(target) + blocks // 2) % blocks
    return jnp.where((block_of(source) == first) | (block_of(source) == other_side), factor * entries, entries)


def level_of(key, dims, shards, low, top_value):
    def one(position, parts):
        steps = jax.random.uniform(jax.random.fold_in(jax.random.fold_in(key, 6), position), (parts,), jnp.float32, low / len(shards), top_value / len(shards))
        return jnp.repeat(jnp.exp(steps), dims[position] // parts).reshape((-1,) + (1,) * (len(dims) - position - 1))

    factor_of = one(*shards[0])
    for cut in shards[1:]:
        factor_of = factor_of * one(*cut)
    return factor_of


def shared_out(key, own, number, rows, count, top, limit, skew):
    ranking = jax.random.permutation(key, count)
    heavy_load, usual = shares(count, rows * top, limit, skew, True), shares(count, rows * top, limit, skew, False)
    places = jnp.arange(count)

    def named(lengths, offset_by):
        used = int((lengths > 0).sum())
        fixed = max(1, used // 4)
        shifted = fixed + (places - fixed + offset_by * (used - fixed)) % max(1, count - fixed)
        return jnp.zeros((count,), jnp.int32).at[ranking[jnp.where(places < fixed, places, shifted)]].set(jnp.asarray(lengths, jnp.int32))

    lengths = jnp.where(number % 4 == 0, named(heavy_load, number // 4), named(usual, number - number // 4 - 1))
    mixed = jax.random.permutation(jax.random.fold_in(own, 3), count)
    donor, receiver = mixed[0:count // 2 * 2:2], mixed[1:count // 2 * 2:2]
    margin = jnp.minimum(lengths[donor] - 1, limit - lengths[receiver]) // 2
    margin = jnp.where((donor == ranking[0]) | (receiver == ranking[0]) | (lengths[receiver] == 0), 0, jnp.maximum(margin, 0))
    shifted = jax.random.randint(jax.random.fold_in(own, 4), (count // 2,), 0, 1 << 20) % (margin + 1)
    lengths = lengths.at[donor].add(-shifted).at[receiver].add(shifted)
    labels = jnp.searchsorted(jnp.cumsum(lengths), jnp.arange(rows * top), side="right").astype(jnp.int32)
    table = labels.reshape(top, rows).T
    table = table[jax.random.permutation(jax.random.fold_in(own, 1), rows)]
    offset_by = jax.random.randint(jax.random.fold_in(own, 2), (rows, 1), 0, top)
    return jnp.take_along_axis(table, (jnp.arange(top)[None, :] + offset_by) % top, axis=1)


def shares(number_of, total, most, lean, full):
    portions = [(1 << 20) // math.isqrt(standing ** lean) + 1 for standing in range(1, number_of + 1)]
    largest = most if full else min(most, max(-(-total // number_of), total * portions[0] // sum(portions)))
    least = 1 if total - largest >= number_of - 1 else 0
    counts, spare = [largest] + [least] * (number_of - 1), total - largest - least * (number_of - 1)
    while spare > 0:
        free = [i for i in range(1, number_of) if counts[i] < largest] or [i for i in range(1, number_of) if counts[i] < most]
        mass, left = sum([portions[i] for i in free]), spare
        for i in free:
            extra = min(most - counts[i], max(1, left * portions[i] // mass), spare)
            counts[i] = counts[i] + extra
            spare = spare - extra
    return np.array(counts)


def gaussian(stream_key, dims, scale, most, cuts=(), held_as=jnp.bfloat16):
    gain = level_of(stream_key, dims, cuts, -0.22, 0.18) if cuts else 1.0
    values = jax.random.normal(stream_key, dims, jnp.float32) * scale * gain
    return jnp.minimum(jnp.maximum(values, -most), most).astype(held_as)


def noise_with(rng, shape, spread, most, pieces, heavy, kind=jnp.bfloat16):
    array = spread * jax.random.normal(rng, shape, jnp.float32)
    if pieces:
        array = array * level_of(rng, shape, pieces, -0.22, 0.18)
    return jnp.clip(raised(array, jax.random.fold_in(rng, 3), *heavy), -most, most).astype(kind)


def setup_inputs(seed: int = 0) -> dict:
    key_list = jax.random.split(jax.random.key(seed), 11)
    queries = draw_queries(jax.random.fold_in(key_list[10], 71), 0)
    cache_kv = draw_cache_kv(jax.random.fold_in(key_list[10], 71), 0)
    block_kv = gaussian(key_list[2], (2, SEQS_ALL, MASKED, KVH * HD), 1.0, 6.0, ((1, 16), (2, 16)))
    stream_in = draw_stream_in(jax.random.fold_in(key_list[10], 71), 0)
    out_proj = noise_with(key_list[4], (H * HD, D), (H * HD // 4) ** -0.5, 0.25, ((0, 16),), (0, 1, 16, 2.0))
    norm_gain = jnp.clip(1.0 + 0.18 * jax.random.normal(key_list[5], (D,), jnp.float32), 0.1, 1.9)
    expert_ids_keys = jax.random.split(jax.random.fold_in(key_list[6], 1), ROWS // ROWS_G)
    expert_ids_turns = jax.random.permutation(jax.random.fold_in(key_list[6], 3), ROWS // ROWS_G)
    expert_ids = jax.vmap(lambda own, number: shared_out(jax.random.fold_in(key_list[6], 2), own, number, ROWS_G, EXPERTS, TOP, CAP, 2))(expert_ids_keys, expert_ids_turns).reshape((ROWS, TOP))
    gate_weights = jnp.clip(jnp.exp(math.log(0.3) - 2.3025852 * jax.random.uniform(key_list[7], (ROWS, TOP), jnp.float32) ** level_of(key_list[7], (ROWS, TOP), ((0, 16),), -0.2, 0.2)), 0.03, 0.3)
    expert_in = gaussian(key_list[8], (2, N_EXP, D, OWNED * EW), D ** -0.5, 0.09375, ((1, 16), (3, 16)))
    expert_out = noise_with(key_list[9], (N_EXP, OWNED * EW, D), EW ** -0.5, 0.375, ((0, 16), (1, 16)), (1, 2, 16, 2.0))
    return dict(queries=queries, cache_kv=cache_kv, block_kv=block_kv, stream_in=stream_in, out_proj=out_proj, norm_gain=norm_gain, expert_ids=expert_ids, gate_weights=gate_weights, expert_in=expert_in, expert_out=expert_out)


def attend(items):
    query_rows, cache_pair, block_pair = items
    group = H // KVH
    all_keys = jnp.concatenate([cache_pair[0], block_pair[0]], axis=0).astype(jnp.float32).reshape(-1, KVH, HD)
    values = jnp.concatenate([cache_pair[1], block_pair[1]], axis=0).astype(jnp.float32).reshape(-1, KVH, HD)
    query_heads = query_rows.astype(jnp.float32).reshape(MASKED, KVH, group, HD)
    scores = jnp.einsum('mkgd,nkd->mkgn', query_heads, all_keys) * HD ** (-0.5)
    row_peak = lax.optimization_barrier(jnp.max(scores, axis=-1, keepdims=True))
    weights = jnp.exp(scores - row_peak)
    row_total = lax.optimization_barrier(jnp.sum(weights, axis=-1))
    rounded = lax.optimization_barrier(weights.astype(jnp.bfloat16)).astype(jnp.float32)
    summed = jnp.einsum('mkgn,nkd->mkgd', rounded, values) / row_total[..., None]
    return summed.reshape(MASKED, H * HD).astype(jnp.bfloat16)

def reference(queries, cache_kv, block_kv, stream_in, out_proj, norm_gain, expert_ids, gate_weights, expert_in, expert_out):
    query_seqs = queries.reshape(SEQS_ALL, MASKED, H * HD)
    attended = lax.map(attend, (query_seqs, jnp.moveaxis(cache_kv, 1, 0), jnp.moveaxis(block_kv, 1, 0)))
    attended = attended.reshape(ROWS, H * HD)
    projected = jnp.dot(attended, out_proj, preferred_element_type=jnp.float32)
    stream = (stream_in.astype(jnp.float32) + projected).astype(jnp.bfloat16)
    widened = stream.astype(jnp.float32)
    inverse = lax.rsqrt(lax.optimization_barrier(jnp.mean(widened * widened, axis=1, keepdims=True)) + 1e-06)
    normed = (widened * inverse * norm_gain).astype(jnp.bfloat16)
    slots_max = N_EXP * CAP
    zero_index = jnp.zeros((), jnp.int32)

    def serve_rows(running, expert):
        owner_col = (expert // OWNED).astype(jnp.int32)
        first_col = (expert % OWNED * EW).astype(jnp.int32)
        w_gate = lax.dynamic_slice(expert_in[0], (owner_col, zero_index, first_col), (1, D, EW))[0]
        w_up = lax.dynamic_slice(expert_in[1], (owner_col, zero_index, first_col), (1, D, EW))[0]
        w_down = lax.dynamic_slice(expert_out, (owner_col, first_col, zero_index), (1, EW, D))[0]
        weight = lax.optimization_barrier(jnp.sum(jnp.where(expert_ids == expert, gate_weights, jnp.zeros_like(gate_weights)), axis=1))
        chosen = weight > 0.0
        picked = jnp.nonzero(chosen, size=slots_max, fill_value=0)[0].astype(jnp.int32)
        row_count = jnp.sum(chosen.astype(jnp.int32))
        is_live = jnp.arange(slots_max, dtype=jnp.int32) < row_count
        row_block = normed[picked]
        gate_part = jnp.dot(row_block, w_gate, preferred_element_type=jnp.float32)
        up_part = jnp.dot(row_block, w_up, preferred_element_type=jnp.float32)
        hidden_act = (jax.nn.silu(gate_part) * up_part).astype(jnp.bfloat16)
        result = jnp.dot(hidden_act, w_down, preferred_element_type=jnp.float32)
        factor = jnp.where(is_live, weight[picked], jnp.zeros_like(weight[picked]))
        return (running.at[picked].add(result * factor[:, None]), None)
    expert_sum, unused_out = lax.scan(serve_rows, jnp.zeros((ROWS, D), jnp.float32), jnp.arange(EXPERTS, dtype=jnp.int32))
    return (stream.astype(jnp.float32) + expert_sum).astype(jnp.bfloat16)
```

```python
import functools
import math

import jax
import jax.numpy as jnp
from jax import lax
from jax.experimental import pallas as pl
from jax.experimental.pallas import tpu as pltpu
from jax.sharding import PartitionSpec as P

HD = 128
SLOTS = 16
MESH = pl.DeviceIdType.MESH
F32 = jnp.float32
BF16 = jnp.bfloat16
VMEM_LIMIT = 60 * 1024 * 1024


def dot(a, b):
    return jnp.dot(a, b, preferred_element_type=F32)


def remote(src, dst, send_sem, recv_sem, **where):
    return pltpu.make_async_remote_copy(
        src_ref=src,
        dst_ref=dst,
        send_sem=send_sem,
        recv_sem=recv_sem,
        device_id=where,
        device_id_type=MESH,
    )


def wait_for(ref, sem):
    pltpu.make_async_copy(ref, ref, sem).wait()


def blk(index, size):
    return pl.ds(pl.multiple_of(index * size, size), size)


def nearest(step, here, count):
    odd = step % 2
    return (here + odd * ((step + 1) // 2) + (1 - odd) * (count - step // 2)) % count


def attention_kernel(
    dims,
    q_hbm,
    cache_hbm,
    block_ref,
    stream_hbm,
    proj_hbm,
    out_ref,
    q,
    kv,
    sin,
    wo,
    wo_pair,
    stat,
    stat_pair,
    own_o,
    pair_out,
    pair_in,
    z_out,
    z_in,
    zs_out,
    zs_in,
    att,
    att_pair,
    c_out,
    c_in,
    load_sem,
    wo_load,
    wo_send,
    wo_recv,
    stat_send,
    stat_recv,
    pair_send,
    pair_recv,
    z_send,
    z_recv,
    zs_send,
    zs_recv,
    att_send,
    att_recv,
    c_send,
    c_recv,
):
    nz, ng, seqs, masked, group, cw = dims
    ctx = lax.axis_index("ctx")
    z, core = ctx // 2, ctx % 2
    pair = 2 * z + 1 - core
    rows = seqs * masked
    factor = HD**-0.5 * math.log2(math.e)

    loads = [
        pltpu.make_async_copy(q_hbm, q, load_sem.at[0]),
        pltpu.make_async_copy(cache_hbm, kv, load_sem.at[1]),
        pltpu.make_async_copy(stream_hbm.at[:, blk(ctx, cw)], sin, load_sem.at[2]),
    ]
    for copy in loads:
        copy.start()
    for b in range(nz):
        pltpu.make_async_copy(
            proj_hbm.at[:, blk(2 * b + core, cw)], wo.at[b], wo_load
        ).start()

    barrier = pltpu.get_barrier_semaphore()
    pl.semaphore_signal(barrier, inc=1, device_id={"ctx": pair}, device_id_type=MESH)
    for t in range(1, nz):
        there = 2 * ((z + t) % nz) + core
        pl.semaphore_signal(barrier, inc=1, device_id={"ctx": there}, device_id_type=MESH)
    pl.semaphore_wait(barrier, nz)

    for b in range(nz):
        remote(
            proj_hbm.at[:, blk(2 * b + 1 - core, cw)], wo_pair.at[b], wo_send, wo_recv, ctx=pair
        ).start()

    for copy in loads:
        copy.wait()

    lane = lax.broadcasted_iota(jnp.int32, (masked, 128), 1)

    def attend(i):
        j = (z // 2 + i) % ng
        for s in range(seqs):
            here = pl.ds(s * masked, masked)
            keys = kv[0, s, :, blk(j, HD)]
            values = kv[1, s, :, blk(j, HD)]
            block_keys = block_ref[0, s, :, blk(j, HD)].astype(F32)
            block_values = block_ref[1, s, :, blk(j, HD)].astype(F32)
            heads = []
            for side in range(2):
                part = core + side - 2 * core * side
                for n in range(group // 2):
                    heads.append(j * group + (n // 2) * 4 + 2 * part + n % 2)
            qs = jnp.concatenate([q[here, blk(h, HD)] for h in heads], axis=0)
            scores = (
                lax.dot_general(
                    qs, keys, (((1,), (1,)), ((), ())), preferred_element_type=F32
                )
                * factor
            )
            qf = qs.astype(F32)
            peak = jnp.max(scores, axis=1, keepdims=True)
            extra = []
            for n in range(block_keys.shape[0]):
                e = jnp.sum(qf * block_keys[n : n + 1], axis=1, keepdims=True) * factor
                extra.append(e)
                peak = jnp.maximum(peak, e)
            weights = jnp.exp2(scores - peak)
            total = jnp.sum(weights, axis=1, keepdims=True)
            summed = dot(weights.astype(BF16), values)
            for n in range(block_keys.shape[0]):
                w = jnp.exp2(extra[n] - peak)
                total = total + w
                summed = summed + w.astype(BF16).astype(F32) * block_values[n : n + 1]
            stats = jnp.zeros((masked, 128), F32)
            for n in range(group):
                side, zz, h = n // 4, (n % 4) // 2, n % 2
                cut = slice(n * masked, (n + 1) * masked)
                at = side * 16 + zz * 8 + h
                stats = jnp.where(lane == at, peak[cut], stats)
                stats = jnp.where(lane == at + 2, total[cut], stats)
                place = pl.ds((n % 4) * HD, HD)
                if side == 0:
                    own_o[i, here, place] = summed[cut]
                else:
                    pair_out[i, here, place] = summed[cut].astype(BF16)
            stat[i, here, :] = stats
        remote(
            pair_out.at[i], pair_in.at[i], pair_send.at[i], pair_recv.at[i], ctx=pair
        ).start()
        remote(
            stat.at[i], stat_pair.at[i], stat_send.at[i], stat_recv.at[i], ctx=pair
        ).start()

    lane_all = lax.broadcasted_iota(jnp.int32, (rows, 128), 1)

    def merge(i):
        j = (z // 2 + i) % ng
        wait_for(pair_in.at[i], pair_recv.at[i])
        wait_for(stat_pair.at[i], stat_recv.at[i])
        mine, theirs = stat[i], stat_pair[i]
        merged = jnp.zeros((rows, 128), F32)
        for zz in range(2):
            for h in range(2):
                at = zz * 8 + h
                m0, m1 = mine[:, at : at + 1], theirs[:, at + 16 : at + 17]
                l0, l1 = mine[:, at + 2 : at + 3], theirs[:, at + 18 : at + 19]
                peak = jnp.maximum(m0, m1)
                f0, f1 = jnp.exp2(m0 - peak), jnp.exp2(m1 - peak)
                merged = jnp.where(lane_all == at, peak, merged)
                merged = jnp.where(lane_all == at + 2, l0 * f0 + l1 * f1, merged)
                place = pl.ds((zz * 2 + h) * HD, HD)
                both = own_o[i, :, place] * f0 + pair_in[i, :, place].astype(F32) * f1
                z_out[2 * j + zz, :, pl.ds(h * HD, HD)] = both.astype(BF16)
        turned = merged.T
        for zz in range(2):
            there = 2 * j + zz
            zs_out[there] = turned[zz * 8 : zz * 8 + 8]

            @pl.when(there == z)
            def _():
                z_in[there] = z_out[there]
                zs_in[there] = zs_out[there]

            @pl.when(there != z)
            def _():
                remote(
                    z_out.at[there],
                    z_in.at[z],
                    z_send.at[there],
                    z_recv.at[z],
                    ctx=2 * there + core,
                ).start()
                remote(
                    zs_out.at[there],
                    zs_in.at[z],
                    zs_send.at[there],
                    zs_recv.at[z],
                    ctx=2 * there + core,
                ).start()

    attend(0)

    def turn(i, carry):
        attend(i)
        merge(i - 1)
        return carry

    lax.fori_loop(1, ng, turn, 0)
    merge(ng - 1)

    for t in range(1, nz):
        source = (z + t) % nz
        wait_for(z_in.at[source], z_recv.at[source])
        wait_for(zs_in.at[source], zs_recv.at[source])
    turned = jnp.concatenate([zs_in[b] for b in range(nz)], axis=0).T
    for h in range(2):
        peaks = [turned[:, 8 * b + h : 8 * b + h + 1] for b in range(nz)]
        peak = functools.reduce(jnp.maximum, peaks)
        total = jnp.zeros((rows, 1), F32)
        summed = jnp.zeros((rows, HD), F32)
        for b in range(nz):
            f = jnp.exp2(peaks[b] - peak)
            total = total + turned[:, 8 * b + h + 2 : 8 * b + h + 3] * f
            summed = summed + z_in[b, :, pl.ds(h * HD, HD)].astype(F32) * f
        att[:, pl.ds(h * HD, HD)] = (summed / total).astype(BF16)
    swap = remote(att, att_pair, att_send, att_recv, ctx=pair)
    swap.start()
    for b in range(nz):
        pltpu.make_async_copy(
            proj_hbm.at[:, blk(2 * b + core, cw)], wo.at[b], wo_load
        ).wait()
    wait_for(wo_pair, wo_recv)
    swap.wait_recv()
    mine, theirs = att[...], att_pair[...]
    for t in range(1, nz):
        there = nearest(t, z, nz)
        c_out[there] = (dot(mine, wo[there]) + dot(theirs, wo_pair[there])).astype(BF16)
        remote(
            c_out.at[there], c_in.at[z], c_send.at[there], c_recv.at[z], ctx=2 * there + core
        ).start()
    total = dot(mine, wo[z]) + dot(theirs, wo_pair[z]) + sin[...].astype(F32)
    for t in range(1, nz):
        source = nearest(t, z, nz)
        wait_for(c_in.at[source], c_recv.at[source])
        total = total + c_in[source].astype(F32)
    out_ref[...] = total.astype(BF16)

    swap.wait_send()
    wait_for(wo_pair, wo_send)
    for i in range(ng):
        wait_for(pair_out.at[i], pair_send.at[i])
        wait_for(stat.at[i], stat_send.at[i])
    for t in range(1, nz):
        there = (z + t) % nz
        wait_for(z_out.at[there], z_send.at[there])
        wait_for(zs_out.at[there], zs_send.at[there])
        wait_for(c_out.at[there], c_send.at[there])


def expert_kernel(
    dims,
    stream_ref,
    ids_ref,
    gates_ref,
    gain_ref,
    in_hbm,
    down_hbm,
    out_ref,
    w_in,
    wd,
    wd_pair,
    blocks,
    place,
    combine,
    d_out,
    d_in,
    d_pair,
    squares,
    acc,
    act,
    act_pair,
    r_out,
    r_in,
    f_out,
    f_in,
    in_load,
    wd_load,
    wd_send,
    wd_recv,
    g_send,
    g_recv,
    d_send,
    d_recv,
    p_send,
    p_recv,
    act_send,
    act_recv,
    r_send,
    r_recv,
    f_send,
    f_recv,
):
    nz, ne, grid, rows, cw, hw = dims
    ctx, e = lax.axis_index("ctx"), lax.axis_index("exp")
    z, core = ctx // 2, ctx % 2
    pair = 2 * z + 1 - core
    slots = ne * SLOTS
    ny = grid[1]
    ex, ey = e // ny, e % ny
    peers = []
    for t in range(1, ne):
        peers.append(((ex + t // ny) % grid[0]) * ny + (ey + t % ny) % ny)

    load_in = pltpu.make_async_copy(in_hbm.at[:, 0], w_in, in_load)
    load_in.start()
    for b in range(nz):
        pltpu.make_async_copy(
            down_hbm.at[0, :, blk(2 * b + core, cw)], wd.at[b], wd_load
        ).start()

    barrier = pltpu.get_barrier_semaphore()
    pl.semaphore_signal(barrier, inc=1, device_id={"ctx": pair}, device_id_type=MESH)
    for t in range(1, nz):
        there = 2 * ((z + t) % nz) + core
        pl.semaphore_signal(barrier, inc=1, device_id={"ctx": there}, device_id_type=MESH)
    for peer in peers:
        pl.semaphore_signal(barrier, inc=1, device_id={"exp": peer}, device_id_type=MESH)
    pl.semaphore_wait(barrier, nz + ne - 1)

    for t in range(1, nz):
        there = nearest(t, z, nz)
        remote(
            stream_ref, blocks.at[z], g_send.at[there], g_recv.at[z], ctx=2 * there + core
        ).start()
    for b in range(nz):
        remote(
            down_hbm.at[0, :, blk(2 * b + 1 - core, cw)],
            wd_pair.at[b],
            wd_send,
            wd_recv,
            ctx=pair,
        ).start()
    blocks[z] = stream_ref[...]

    lane = lax.broadcasted_iota(jnp.int32, (rows, slots), 1)
    wanted = (lane // SLOTS) * nz + z
    hit = jnp.zeros((rows, slots), F32)
    weight = jnp.zeros((rows, slots), F32)
    ids, gates = ids_ref[...], gates_ref[...]
    for t in range(ids.shape[1]):
        same = ids[:, t : t + 1] == wanted
        hit = jnp.where(same, 1.0, hit)
        weight = jnp.where(same, gates[:, t : t + 1], weight)
    below = lax.broadcasted_iota(jnp.int32, (rows, rows), 1) < lax.broadcasted_iota(
        jnp.int32, (rows, rows), 0
    )
    rank = dot(below.astype(F32).astype(BF16), hit.astype(BF16))
    placed = jnp.where(rank == (lane % SLOTS).astype(F32), hit, 0.0)
    combine[...] = (placed * weight).astype(BF16)
    place[...] = placed.T.astype(BF16)
    squares[...] = jnp.zeros_like(squares)
    acc[...] = jnp.zeros_like(acc)

    def dispatch(t):
        b = nearest(t, z, nz)

        @pl.when(t > 0)
        def _():
            wait_for(blocks.at[b], g_recv.at[b])

        d_out[b] = dot(place[...], blocks[b]).astype(BF16)
        for peer in peers:
            remote(
                d_out.at[b, blk(peer, SLOTS)],
                d_in.at[b, blk(e, SLOTS)],
                d_send.at[b],
                d_recv.at[b],
                exp=peer,
            ).start()
        d_in[b, blk(e, SLOTS)] = d_out[b, blk(e, SLOTS)]

    def feed(rows_in, column):
        wide = rows_in.astype(F32)
        squared = wide * wide
        part = squares[...]
        for n in range(cw // 128):
            part = part + squared[:, n * 128 : (n + 1) * 128]
        squares[...] = part
        scaled = (wide * gain_ref[:, blk(column, cw)]).astype(BF16)
        for half in range(2):
            at = pl.ds(half * hw, hw)
            acc[:, at] = acc[:, at] + dot(scaled, w_in[half, blk(column, cw), :])

    def take(t):
        b = nearest(t, z, nz)
        got = pl.ds(0, slots - SLOTS)
        wait_for(d_in.at[b, got], d_recv.at[b])
        remote(d_in.at[b], d_pair.at[b], p_send.at[b], p_recv.at[b], ctx=pair).start()
        feed(d_in[b], 2 * b + core)

    def take_pair(t):
        b = nearest(t, z, nz)
        wait_for(d_pair.at[b], p_recv.at[b])
        feed(d_pair[b], 2 * b + 1 - core)

    lag = min(2, nz - 1)

    def lead(t, carry):
        dispatch(t)
        return carry

    lax.fori_loop(0, lag, lead, 0)
    load_in.wait()

    def turn(t, carry):
        @pl.when(t < nz)
        def _():
            dispatch(t)

        @pl.when(t < nz + lag)
        def _():
            take(t - lag)

        @pl.when(t > lag)
        def _():
            take_pair(t - lag - 1)

        return carry

    lax.fori_loop(lag, nz + lag + 1, turn, 0)

    mean = jnp.sum(squares[...], axis=1, keepdims=True) * (1.0 / (2 * nz * cw))
    inverse = lax.rsqrt(mean + 1e-6)
    gate = acc[:, pl.ds(0, hw)] * inverse
    up = acc[:, pl.ds(hw, hw)] * inverse
    act[...] = (gate / (1.0 + jnp.exp(-gate)) * up).astype(BF16)
    swap = remote(act, act_pair, act_send, act_recv, ctx=pair)
    swap.start()
    for b in range(nz):
        pltpu.make_async_copy(
            down_hbm.at[0, :, blk(2 * b + core, cw)], wd.at[b], wd_load
        ).wait()
    wait_for(wd_pair, wd_recv)
    swap.wait_recv()

    def give(t):
        b = nearest((t + 1) % nz, z, nz)
        r_out[b] = (dot(act[...], wd[b]) + dot(act_pair[...], wd_pair[b])).astype(BF16)
        for peer in peers:
            remote(
                r_out.at[b, blk(peer, SLOTS)],
                r_in.at[b, blk(e, SLOTS)],
                r_send.at[b],
                r_recv.at[b],
                exp=peer,
            ).start()
        r_in[b, blk(e, SLOTS)] = r_out[b, blk(e, SLOTS)]

    def join(t):
        b = nearest((t + 1) % nz, z, nz)
        wait_for(r_in.at[b, pl.ds(0, slots - SLOTS)], r_recv.at[b])
        f_out[b] = dot(combine[...], r_in[b]).astype(BF16)

        @pl.when(b != z)
        def _():
            remote(
                f_out.at[b], f_in.at[z], f_send.at[b], f_recv.at[z], ctx=2 * b + core
            ).start()

    def lead_back(t, carry):
        give(t)
        return carry

    lax.fori_loop(0, lag, lead_back, 0)

    def turn_back(t, carry):
        @pl.when(t < nz)
        def _():
            give(t)

        join(t - lag)
        return carry

    lax.fori_loop(lag, nz + lag, turn_back, 0)

    total = f_out[z].astype(F32)
    for t in range(1, nz):
        source = nearest(t, z, nz)
        wait_for(f_in.at[source], f_recv.at[source])
        total = total + f_in[source].astype(F32)
    out_ref[...] = (stream_ref[...].astype(F32) + total).astype(BF16)

    swap.wait_send()
    wait_for(wd_pair, wd_send)
    got = pl.ds(0, slots - SLOTS)
    for b in range(nz):
        wait_for(d_out.at[b, got], d_send.at[b])
        wait_for(r_out.at[b, got], r_send.at[b])
        wait_for(d_in.at[b], p_send.at[b])
    for t in range(1, nz):
        there = (z + t) % nz
        wait_for(blocks.at[there], g_send.at[there])
        wait_for(f_out.at[there], f_send.at[there])


def body(
    queries,
    cache_kv,
    block_kv,
    stream_in,
    out_proj,
    norm_gain,
    expert_ids,
    gate_weights,
    expert_in,
    expert_out,
):
    ctx_size, ne = lax.axis_size("ctx"), lax.axis_size("exp")
    nz = ctx_size // 2
    rows, width = queries.shape
    seqs = cache_kv.shape[1]
    masked = rows // seqs
    kvh = cache_kv.shape[3] // HD
    group = width // HD // kvh
    ng, cw, hw = kvh, width // ctx_size, expert_in.shape[3]
    slots = ne * SLOTS
    grid = (4, 4) if ne == 16 else (1, ne)
    dma, anyspace, vmem = (
        pltpu.SemaphoreType.DMA,
        pl.BlockSpec(memory_space=pl.ANY),
        pl.BlockSpec(memory_space=pltpu.VMEM),
    )
    V = pltpu.VMEM
    stream = pl.pallas_call(
        functools.partial(attention_kernel, (nz, ng, seqs, masked, group, cw)),
        out_shape=jax.ShapeDtypeStruct((rows, cw), BF16),
        in_specs=[anyspace, anyspace, vmem, anyspace, anyspace],
        out_specs=vmem,
        scratch_shapes=[
            V((rows, width), BF16),
            V(cache_kv.shape, BF16),
            V((rows, cw), BF16),
            V((nz, 2 * HD, cw), BF16),
            V((nz, 2 * HD, cw), BF16),
            V((ng, rows, 128), F32),
            V((ng, rows, 128), F32),
            V((ng, rows, 4 * HD), F32),
            V((ng, rows, 4 * HD), BF16),
            V((ng, rows, 4 * HD), BF16),
            V((nz, rows, 2 * HD), BF16),
            V((nz, rows, 2 * HD), BF16),
            V((nz, 8, rows), F32),
            V((nz, 8, rows), F32),
            V((rows, 2 * HD), BF16),
            V((rows, 2 * HD), BF16),
            V((nz, rows, cw), BF16),
            V((nz, rows, cw), BF16),
            dma((3,)),
            dma(()),
            dma(()),
            dma(()),
            dma((ng,)),
            dma((ng,)),
            dma((ng,)),
            dma((ng,)),
            dma((nz,)),
            dma((nz,)),
            dma((nz,)),
            dma((nz,)),
            dma(()),
            dma(()),
            dma((nz,)),
            dma((nz,)),
        ],
        compiler_params=pltpu.CompilerParams(
            collective_id=1, has_side_effects=True, vmem_limit_bytes=VMEM_LIMIT
        ),
    )(queries, cache_kv, block_kv, stream_in, out_proj)
    return pl.pallas_call(
        functools.partial(expert_kernel, (nz, ne, grid, rows, cw, hw)),
        out_shape=jax.ShapeDtypeStruct((rows, cw), BF16),
        in_specs=[vmem, vmem, vmem, vmem, anyspace, anyspace],
        out_specs=vmem,
        scratch_shapes=[
            V((2, width, hw), BF16),
            V((nz, hw, cw), BF16),
            V((nz, hw, cw), BF16),
            V((nz, rows, cw), BF16),
            V((slots, rows), BF16),
            V((rows, slots), BF16),
            V((nz, slots, cw), BF16),
            V((nz, slots, cw), BF16),
            V((nz, slots, cw), BF16),
            V((slots, 128), F32),
            V((slots, 2 * hw), F32),
            V((slots, hw), BF16),
            V((slots, hw), BF16),
            V((nz, slots, cw), BF16),
            V((nz, slots, cw), BF16),
            V((nz, rows, cw), BF16),
            V((nz, rows, cw), BF16),
            dma(()),
            dma(()),
            dma(()),
            dma(()),
            dma((nz,)),
            dma((nz,)),
            dma((nz,)),
            dma((nz,)),
            dma((nz,)),
            dma((nz,)),
            dma(()),
            dma(()),
            dma((nz,)),
            dma((nz,)),
            dma((nz,)),
            dma((nz,)),
        ],
        compiler_params=pltpu.CompilerParams(
            collective_id=2, has_side_effects=True, vmem_limit_bytes=VMEM_LIMIT
        ),
    )(stream, expert_ids, gate_weights, norm_gain.reshape(1, width), expert_in, expert_out)


def solution(mesh):
    placed = (
        P("exp", None),
        P(None, "exp", "ctx", None),
        P(None, "exp", "ctx", None),
        P("exp", None),
        P("ctx", None),
        P(),
        P("exp", None),
        P("exp", None),
        P(None, "exp", None, "ctx"),
        P("exp", "ctx", None),
    )
    return jax.shard_map(
        body, mesh=mesh, in_specs=placed, out_specs=P("exp", "ctx"), check_vma=False
    )
```

```python
import functools
import math

import jax
import jax.numpy as jnp
from jax import lax
from jax.experimental import pallas as pl
from jax.experimental.pallas import tpu as pltpu
from jax.sharding import PartitionSpec as P

HD = 128
SLOTS = 16
PARTS = 2
MESH = pl.DeviceIdType.MESH
F32 = jnp.float32
BF16 = jnp.bfloat16
VMEM_LIMIT = 60 * 1024 * 1024


def dot(a, b):
    return jnp.dot(a, b, preferred_element_type=F32)


def remote(src, dst, send_sem, recv_sem, **where):
    return pltpu.make_async_remote_copy(
        src_ref=src,
        dst_ref=dst,
        send_sem=send_sem,
        recv_sem=recv_sem,
        device_id=where,
        device_id_type=MESH,
    )


def wait_for(ref, sem):
    pltpu.make_async_copy(ref, ref, sem).wait()


def blk(index, size):
    return pl.ds(pl.multiple_of(index * size, size), size)


def nearest(step, here, count):
    odd = step % 2
    return (here + odd * ((step + 1) // 2) + (1 - odd) * (count - step // 2)) % count


def layer_kernel(
    dims,
    q_hbm,
    cache_hbm,
    block_ref,
    stream_hbm,
    proj_hbm,
    gain_ref,
    ids_ref,
    gates_ref,
    in_hbm,
    down_hbm,
    out_ref,
    q,
    kv,
    sin,
    wo,
    w_in,
    wd,
    stat,
    stat_pair,
    own_o,
    pair_out,
    pair_in,
    z_out,
    z_in,
    zs_out,
    zs_in,
    att,
    c_out,
    c_in,
    stream,
    blocks,
    place,
    combine,
    d_out,
    d_in,
    squares,
    acc,
    act,
    r_out,
    r_in,
    f_out,
    f_in,
    q_load,
    kv_load,
    sin_load,
    wo_load,
    wo_send,
    wo_recv,
    in_load,
    wd_load,
    wd_send,
    wd_recv,
    stat_send,
    stat_recv,
    pair_send,
    pair_recv,
    z_send,
    z_recv,
    zs_send,
    zs_recv,
    att_send,
    att_recv,
    c_send,
    c_recv,
    g_send,
    g_recv,
    d_send,
    d_recv,
    p_send,
    p_recv,
    act_send,
    act_recv,
    r_send,
    r_recv,
    f_send,
    f_recv,
):
    nz, ng, ne, grid, seqs, masked, group, cw, hw = dims
    ctx, e = lax.axis_index("ctx"), lax.axis_index("exp")
    z, core = ctx // 2, ctx % 2
    pair = 2 * z + 1 - core
    rows = seqs * masked
    span = seqs // PARTS
    pr = rows // PARTS
    steps = PARTS * ng
    slots = ne * SLOTS
    mine = blk(core, cw)
    factor = HD**-0.5 * math.log2(math.e)
    ny = grid[1]
    ex, ey = e // ny, e % ny
    peers = []
    for t in range(1, ne):
        peers.append(((ex + t // ny) % grid[0]) * ny + (ey + t % ny) % ny)

    def part_load(p):
        return (
            pltpu.make_async_copy(
                q_hbm.at[blk(p, pr)], q.at[blk(p, pr)], q_load.at[p]
            ),
            pltpu.make_async_copy(
                cache_hbm.at[:, pl.ds(p * span, span)],
                kv.at[:, pl.ds(p * span, span)],
                kv_load.at[p],
            ),
        )

    for p in range(PARTS):
        for copy in part_load(p):
            copy.start()

    barrier = pltpu.get_barrier_semaphore()
    pl.semaphore_signal(barrier, inc=1, device_id={"ctx": pair}, device_id_type=MESH)
    for t in range(1, nz):
        there = 2 * ((z + t) % nz) + core
        pl.semaphore_signal(barrier, inc=1, device_id={"ctx": there}, device_id_type=MESH)
    for peer in peers:
        pl.semaphore_signal(barrier, inc=1, device_id={"exp": peer}, device_id_type=MESH)

    load_sin = pltpu.make_async_copy(stream_hbm.at[:, blk(ctx, cw)], sin, sin_load)
    load_sin.start()
    for b in range(nz):
        pltpu.make_async_copy(
            proj_hbm.at[:, blk(2 * b + core, cw)], wo.at[b, blk(core, 2 * HD)], wo_load
        ).start()
    for half in range(2):
        pltpu.make_async_copy(
            in_hbm.at[half, 0], w_in.at[:, pl.ds(half * hw, hw)], in_load.at[half]
        ).start()
    for b in range(nz):
        pltpu.make_async_copy(
            down_hbm.at[0, :, blk(2 * b + core, cw)], wd.at[b, blk(core, hw)], wd_load
        ).start()

    pl.semaphore_wait(barrier, nz + ne - 1)

    for b in range(nz):
        remote(
            proj_hbm.at[:, blk(2 * b + 1 - core, cw)],
            wo.at[b, blk(core, 2 * HD)],
            wo_send,
            wo_recv,
            ctx=pair,
        ).start()

    lane = lax.broadcasted_iota(jnp.int32, (masked, 128), 1)

    def attend(k):
        p, i = k // ng, k % ng
        j = (z // 2 + ng // 2 + i) % ng

        @pl.when(i == 0)
        def _():
            for copy in part_load(p):
                copy.wait()

        for n in range(span):
            s = p * span + n
            here = blk(s, masked)
            local = pl.ds(n * masked, masked)
            keys = kv[0, s, :, blk(j, HD)]
            values = kv[1, s, :, blk(j, HD)]
            block_keys = block_ref[0, s, :, blk(j, HD)].astype(F32)
            block_values = block_ref[1, s, :, blk(j, HD)].astype(F32)
            heads = []
            for side in range(2):
                part = core + side - 2 * core * side
                for m in range(group // 2):
                    heads.append(j * group + (m // 2) * 4 + 2 * part + m % 2)
            qs = jnp.concatenate([q[here, blk(h, HD)] for h in heads], axis=0)
            scores = (
                lax.dot_general(
                    qs, keys, (((1,), (1,)), ((), ())), preferred_element_type=F32
                )
                * factor
            )
            qf = qs.astype(F32)
            peak = jnp.max(scores, axis=1, keepdims=True)
            extra = []
            for m in range(block_keys.shape[0]):
                one = jnp.sum(qf * block_keys[m : m + 1], axis=1, keepdims=True) * factor
                extra.append(one)
                peak = jnp.maximum(peak, one)
            weights = jnp.exp2(scores - peak)
            total = jnp.sum(weights, axis=1, keepdims=True)
            summed = dot(weights.astype(BF16), values)
            for m in range(block_keys.shape[0]):
                w = jnp.exp2(extra[m] - peak)
                total = total + w
                summed = summed + w.astype(BF16).astype(F32) * block_values[m : m + 1]
            stats = jnp.zeros((masked, 128), F32)
            for m in range(group):
                side, zz, h = m // 4, (m % 4) // 2, m % 2
                cut = slice(m * masked, (m + 1) * masked)
                at = side * 16 + zz * 8 + h
                stats = jnp.where(lane == at, peak[cut], stats)
                stats = jnp.where(lane == at + 2, total[cut], stats)
                spot = pl.ds((m % 4) * HD, HD)
                if side == 0:
                    own_o[k, local, spot] = summed[cut]
                else:
                    pair_out[k, local, spot] = summed[cut].astype(BF16)
            stat[k, local, :] = stats
        remote(
            pair_out.at[k], pair_in.at[k], pair_send.at[k], pair_recv.at[k], ctx=pair
        ).start()
        remote(
            stat.at[k], stat_pair.at[k], stat_send.at[k], stat_recv.at[k], ctx=pair
        ).start()

    lane_part = lax.broadcasted_iota(jnp.int32, (pr, 128), 1)

    def merge(k):
        p, i = k // ng, k % ng
        j = (z // 2 + ng // 2 + i) % ng
        wait_for(pair_in.at[k], pair_recv.at[k])
        wait_for(stat_pair.at[k], stat_recv.at[k])
        ours, theirs = stat[k], stat_pair[k]
        merged = jnp.zeros((pr, 128), F32)
        for zz in range(2):
            for h in range(2):
                at = zz * 8 + h
                m0, m1 = ours[:, at : at + 1], theirs[:, at + 16 : at + 17]
                l0, l1 = ours[:, at + 2 : at + 3], theirs[:, at + 18 : at + 19]
                peak = jnp.maximum(m0, m1)
                f0, f1 = jnp.exp2(m0 - peak), jnp.exp2(m1 - peak)
                merged = jnp.where(lane_part == at, peak, merged)
                merged = jnp.where(lane_part == at + 2, l0 * f0 + l1 * f1, merged)
                spot = pl.ds((zz * 2 + h) * HD, HD)
                both = own_o[k, :, spot] * f0 + pair_in[k, :, spot].astype(F32) * f1
                z_out[p, 2 * j + zz, :, pl.ds(h * HD, HD)] = both.astype(BF16)
        turned = jnp.concatenate([merged, jnp.zeros((128 - pr, 128), F32)], axis=0).T
        for zz in range(2):
            there = 2 * j + zz
            zs_out[p, there] = turned[zz * 8 : zz * 8 + 8]

            @pl.when(there == z)
            def _():
                z_in[p, there] = z_out[p, there]
                zs_in[p, there] = zs_out[p, there]

            @pl.when(there != z)
            def _():
                remote(
                    z_out.at[p, there],
                    z_in.at[p, z],
                    z_send.at[p, there],
                    z_recv.at[p, z],
                    ctx=2 * there + core,
                ).start()
                remote(
                    zs_out.at[p, there],
                    zs_in.at[p, z],
                    zs_send.at[p, there],
                    zs_recv.at[p, z],
                    ctx=2 * there + core,
                ).start()

    attend(0)

    def turn(k, carry):
        attend(k)
        merge(k - 1)
        return carry

    lax.fori_loop(1, steps, turn, 0)
    merge(steps - 1)

    def finish_heads(p):
        for t in range(1, nz):
            source = (z + t) % nz
            wait_for(z_in.at[p, source], z_recv.at[p, source])
            wait_for(zs_in.at[p, source], zs_recv.at[p, source])
        turned = jnp.concatenate([zs_in[p, b] for b in range(nz)], axis=0).T
        here = pl.ds(p * pr, pr)
        for h in range(2):
            peaks = [turned[:pr, 8 * b + h : 8 * b + h + 1] for b in range(nz)]
            peak = functools.reduce(jnp.maximum, peaks)
            total = jnp.zeros((pr, 1), F32)
            summed = jnp.zeros((pr, HD), F32)
            for b in range(nz):
                f = jnp.exp2(peaks[b] - peak)
                total = total + turned[:pr, 8 * b + h + 2 : 8 * b + h + 3] * f
                summed = summed + z_in[p, b, :, pl.ds(h * HD, HD)].astype(F32) * f
            att[here, blk(2 * core + h, HD)] = (summed / total).astype(BF16)
        return remote(
            att.at[here, mine], att.at[here, mine], att_send.at[p], att_recv.at[p], ctx=pair
        )

    def project(p):
        here = pl.ds(p * pr, pr)
        wait_for(att.at[here, mine], att_recv.at[p])
        heads = att[here, :]
        for t in range(1, nz):
            there = nearest(nz - t, z, nz)
            c_out[p, there] = dot(heads, wo[there]).astype(BF16)
            remote(
                c_out.at[p, there],
                c_in.at[p, z],
                c_send.at[p, there],
                c_recv.at[p, z],
                ctx=2 * there + core,
            ).start()

    def finish_stream(p):
        here = pl.ds(p * pr, pr)
        total = dot(att[here, :], wo[z]) + sin[here, :].astype(F32)
        for t in range(1, nz):
            source = nearest(t, z, nz)
            wait_for(c_in.at[p, source], c_recv.at[p, source])
            total = total + c_in[p, source].astype(F32)
        stream[here, :] = total.astype(BF16)
        for t in range(1, nz):
            there = nearest(t, z, nz)
            remote(
                stream.at[here],
                blocks.at[z, here],
                g_send.at[p, there],
                g_recv.at[p, z],
                ctx=2 * there + core,
            ).start()

    load_sin.wait()
    wait_for(wo.at[:, blk(core, 2 * HD)], wo_load)
    for p in range(PARTS):
        finish_heads(p).start()
        if p == 0:
            wait_for(wo.at[:, blk(core, 2 * HD)], wo_recv)
        project(p)

    for b in range(nz):
        remote(
            down_hbm.at[0, :, blk(2 * b + 1 - core, cw)],
            wd.at[b, blk(core, hw)],
            wd_send,
            wd_recv,
            ctx=pair,
        ).start()
    slot = lax.broadcasted_iota(jnp.int32, (slots, rows), 0)
    wanted = (slot // SLOTS) * nz + z
    hit = jnp.zeros((slots, rows), F32)
    weight = jnp.zeros((slots, rows), F32)
    ids, gates = ids_ref[...], gates_ref[...]
    for t in range(ids.shape[0]):
        same = ids[t : t + 1, :] == wanted
        hit = jnp.where(same, 1.0, hit)
        weight = jnp.where(same, gates[t : t + 1, :], weight)
    earlier = lax.broadcasted_iota(jnp.int32, (rows, rows), 0) < lax.broadcasted_iota(
        jnp.int32, (rows, rows), 1
    )
    rank = dot(hit.astype(BF16), earlier.astype(F32).astype(BF16))
    placed = jnp.where(rank == (slot % SLOTS).astype(F32), hit, 0.0)
    place[...] = placed.astype(BF16)
    combine[...] = (placed * weight).T.astype(BF16)
    squares[...] = jnp.zeros_like(squares)
    acc[...] = jnp.zeros_like(acc)

    for p in range(PARTS):
        finish_stream(p)
    blocks[z] = stream[...]

    def dispatch(t):
        b = nearest(t, z, nz)

        @pl.when(t > 0)
        def _():
            for p in range(PARTS):
                wait_for(blocks.at[b, pl.ds(p * pr, pr)], g_recv.at[p, b])

        d_out[b] = dot(place[...], blocks[b]).astype(BF16)
        for peer in peers:
            remote(
                d_out.at[b, blk(peer, SLOTS)],
                d_in.at[b, blk(e, SLOTS), mine],
                d_send.at[b],
                d_recv.at[b],
                exp=peer,
            ).start()
        d_in[b, blk(e, SLOTS), mine] = d_out[b, blk(e, SLOTS)]

    got = pl.ds(0, slots - SLOTS)

    def take(t):
        b = nearest(t, z, nz)
        wait_for(d_in.at[b, got, mine], d_recv.at[b])
        remote(
            d_in.at[b, :, mine], d_in.at[b, :, mine], p_send.at[b], p_recv.at[b], ctx=pair
        ).start()

    def feed(t):
        b = nearest(t, z, nz)
        wait_for(d_in.at[b, :, mine], p_recv.at[b])
        wide = d_in[b].astype(F32)
        squared = wide * wide
        part = squares[...]
        for n in range(2 * cw // 128):
            part = part + squared[:, n * 128 : (n + 1) * 128]
        squares[...] = part
        scaled = (wide * gain_ref[:, blk(b, 2 * cw)]).astype(BF16)
        acc[...] = acc[...] + dot(scaled, w_in[blk(b, 2 * cw), :])

    lag = min(2, nz - 1)

    def lead(t, carry):
        dispatch(t)
        return carry

    lax.fori_loop(0, lag, lead, 0)
    for half in range(2):
        pltpu.make_async_copy(
            in_hbm.at[half, 0], w_in.at[:, pl.ds(half * hw, hw)], in_load.at[half]
        ).wait()

    def turn_in(t, carry):
        @pl.when(t < nz)
        def _():
            dispatch(t)

        @pl.when(t < nz + lag)
        def _():
            take(t - lag)

        @pl.when(t > lag)
        def _():
            feed(t - lag - 1)

        return carry

    lax.fori_loop(lag, nz + lag + 1, turn_in, 0)

    mean = jnp.sum(squares[...], axis=1, keepdims=True) * (1.0 / (2 * nz * cw))
    inverse = lax.rsqrt(mean + 1e-6)
    gate = acc[:, pl.ds(0, hw)] * inverse
    up = acc[:, pl.ds(hw, hw)] * inverse
    act_mine = act.at[:, blk(core, hw)]
    act[:, blk(core, hw)] = (gate / (1.0 + jnp.exp(-gate)) * up).astype(BF16)
    remote(act_mine, act_mine, act_send, act_recv, ctx=pair).start()
    wait_for(wd.at[:, blk(core, hw)], wd_load)
    wait_for(wd.at[:, blk(core, hw)], wd_recv)
    wait_for(act_mine, act_recv)

    def give(t):
        b = nearest((t + 1) % nz, z, nz)
        r_out[b] = dot(act[...], wd[b]).astype(BF16)
        for peer in peers:
            remote(
                r_out.at[b, blk(peer, SLOTS)],
                r_in.at[b, blk(e, SLOTS)],
                r_send.at[b],
                r_recv.at[b],
                exp=peer,
            ).start()
        r_in[b, blk(e, SLOTS)] = r_out[b, blk(e, SLOTS)]

    def join(t):
        b = nearest((t + 1) % nz, z, nz)
        wait_for(r_in.at[b, got], r_recv.at[b])
        f_out[b] = dot(combine[...], r_in[b]).astype(BF16)

        @pl.when(b != z)
        def _():
            remote(
                f_out.at[b], f_in.at[z], f_send.at[b], f_recv.at[z], ctx=2 * b + core
            ).start()

    def lead_back(t, carry):
        give(t)
        return carry

    lax.fori_loop(0, lag, lead_back, 0)

    def turn_back(t, carry):
        @pl.when(t < nz)
        def _():
            give(t)

        join(t - lag)
        return carry

    lax.fori_loop(lag, nz + lag, turn_back, 0)

    total = f_out[z].astype(F32)
    for t in range(1, nz):
        source = nearest(t, z, nz)
        wait_for(f_in.at[source], f_recv.at[source])
        total = total + f_in[source].astype(F32)
    out_ref[...] = (stream[...].astype(F32) + total).astype(BF16)

    wait_for(wo.at[:, blk(core, 2 * HD)], wo_send)
    wait_for(wd.at[:, blk(core, hw)], wd_send)
    wait_for(act_mine, act_send)

    def drain_pair(k, carry):
        wait_for(pair_out.at[k], pair_send.at[k])
        wait_for(stat.at[k], stat_send.at[k])
        return carry

    lax.fori_loop(0, steps, drain_pair, 0)

    def drain_block(b, carry):
        wait_for(d_out.at[b, got], d_send.at[b])
        wait_for(r_out.at[b, got], r_send.at[b])
        wait_for(d_in.at[b, :, mine], p_send.at[b])
        return carry

    lax.fori_loop(0, nz, drain_block, 0)

    def drain_z(t, carry):
        there = (z + t) % nz
        wait_for(f_out.at[there], f_send.at[there])
        for p in range(PARTS):
            here = pl.ds(p * pr, pr)
            wait_for(z_out.at[p, there], z_send.at[p, there])
            wait_for(zs_out.at[p, there], zs_send.at[p, there])
            wait_for(c_out.at[p, there], c_send.at[p, there])
            wait_for(stream.at[here], g_send.at[p, there])
        return carry

    lax.fori_loop(1, nz, drain_z, 0)
    for p in range(PARTS):
        wait_for(att.at[pl.ds(p * pr, pr), mine], att_send.at[p])


def body(
    queries,
    cache_kv,
    block_kv,
    stream_in,
    out_proj,
    norm_gain,
    expert_ids,
    gate_weights,
    expert_in,
    expert_out,
):
    ctx_size, ne = lax.axis_size("ctx"), lax.axis_size("exp")
    nz = ctx_size // 2
    rows, width = queries.shape
    seqs = cache_kv.shape[1]
    masked = rows // seqs
    ng = cache_kv.shape[3] // HD
    group = width // HD // ng
    cw, hw = width // ctx_size, expert_in.shape[3]
    slots = ne * SLOTS
    grid = (4, 4) if ne == 16 else (1, ne)
    steps, pr = PARTS * ng, rows // PARTS
    dma, vm = pltpu.SemaphoreType.DMA, pltpu.VMEM
    anyspace = pl.BlockSpec(memory_space=pl.ANY)
    vmem = pl.BlockSpec(memory_space=pltpu.VMEM)
    dims = (nz, ng, ne, grid, seqs, masked, group, cw, hw)
    buffers = [
        vm((rows, width), BF16),
        vm(cache_kv.shape, BF16),
        vm((rows, cw), BF16),
        vm((nz, 4 * HD, cw), BF16),
        vm((width, 2 * hw), BF16),
        vm((nz, 2 * hw, cw), BF16),
        vm((steps, pr, 128), F32),
        vm((steps, pr, 128), F32),
        vm((steps, pr, 4 * HD), F32),
        vm((steps, pr, 4 * HD), BF16),
        vm((steps, pr, 4 * HD), BF16),
        vm((PARTS, nz, pr, 2 * HD), BF16),
        vm((PARTS, nz, pr, 2 * HD), BF16),
        vm((PARTS, nz, 8, 128), F32),
        vm((PARTS, nz, 8, 128), F32),
        vm((rows, 4 * HD), BF16),
        vm((PARTS, nz, pr, cw), BF16),
        vm((PARTS, nz, pr, cw), BF16),
        vm((rows, cw), BF16),
        vm((nz, rows, cw), BF16),
        vm((slots, rows), BF16),
        vm((rows, slots), BF16),
        vm((nz, slots, cw), BF16),
        vm((nz, slots, 2 * cw), BF16),
        vm((slots, 128), F32),
        vm((slots, 2 * hw), F32),
        vm((slots, 2 * hw), BF16),
        vm((nz, slots, cw), BF16),
        vm((nz, slots, cw), BF16),
        vm((nz, rows, cw), BF16),
        vm((nz, rows, cw), BF16),
    ]
    counts = [(PARTS,), (PARTS,)] + [()] * 4 + [(2,)] + [()] * 3
    counts += [(steps,)] * 4 + [(PARTS, nz)] * 4 + [(PARTS,)] * 2 + [(PARTS, nz)] * 4
    counts += [(nz,)] * 4 + [()] * 2 + [(nz,)] * 4
    return pl.pallas_call(
        functools.partial(layer_kernel, dims),
        out_shape=jax.ShapeDtypeStruct((rows, cw), BF16),
        in_specs=[anyspace, anyspace, vmem, anyspace, anyspace, vmem, vmem, vmem]
        + [anyspace, anyspace],
        out_specs=vmem,
        scratch_shapes=buffers + [dma(shape) for shape in counts],
        compiler_params=pltpu.CompilerParams(
            collective_id=1, has_side_effects=True, vmem_limit_bytes=VMEM_LIMIT
        ),
    )(
        queries,
        cache_kv,
        block_kv,
        stream_in,
        out_proj,
        norm_gain.reshape(1, width),
        expert_ids.T,
        gate_weights.T,
        expert_in,
        expert_out,
    )


def solution(mesh):
    placed = (
        P("exp", None),
        P(None, "exp", "ctx", None),
        P(None, "exp", "ctx", None),
        P("exp", None),
        P("ctx", None),
        P(),
        P("exp", None),
        P("exp", None),
        P(None, "exp", None, "ctx"),
        P("exp", "ctx", None),
    )
    return jax.shard_map(
        body, mesh=mesh, in_specs=placed, out_specs=P("exp", "ctx"), check_vma=False
    )
```

```python
import functools
import math

import jax
import jax.numpy as jnp
from jax import lax
from jax.experimental import pallas as pl
from jax.experimental.pallas import tpu as pltpu
from jax.sharding import PartitionSpec as P

HD = 128
SLOTS = 16
PARTS = 2
MESH = pl.DeviceIdType.MESH
F32 = jnp.float32
BF16 = jnp.bfloat16
VMEM_LIMIT = 60 * 1024 * 1024


def dot(a, b):
    return jnp.dot(a, b, preferred_element_type=F32)


def dot_t(a, b):
    return lax.dot_general(a, b, (((1,), (1,)), ((), ())), preferred_element_type=F32)


def remote(src, dst, send_sem, recv_sem, **where):
    return pltpu.make_async_remote_copy(
        src_ref=src,
        dst_ref=dst,
        send_sem=send_sem,
        recv_sem=recv_sem,
        device_id=where,
        device_id_type=MESH,
    )


def wait_for(ref, sem):
    pltpu.make_async_copy(ref, ref, sem).wait()


def blk(index, size):
    return pl.ds(pl.multiple_of(index * size, size), size)


def nearest(step, here, count):
    odd = step % 2
    return (here + odd * ((step + 1) // 2) + (1 - odd) * (count - step // 2)) % count


def layer_kernel(
    dims,
    q_hbm,
    cache_hbm,
    block_ref,
    stream_hbm,
    proj_hbm,
    gain_ref,
    ids_ref,
    gates_ref,
    in_hbm,
    down_hbm,
    out_ref,
    q,
    kv,
    kv_pair,
    block,
    sin,
    wo,
    w_in,
    wd,
    stat,
    z_out,
    z_in,
    zs_out,
    zs_in,
    att,
    c_out,
    c_in,
    stream,
    blocks,
    place,
    combine,
    d_out,
    d_in,
    squares,
    acc,
    act,
    r_out,
    r_in,
    f_out,
    f_in,
    q_load,
    kv_load,
    sin_load,
    wo_load,
    wo_send,
    wo_recv,
    in_load,
    wd_load,
    wd_send,
    wd_recv,
    kv_send,
    kv_recv,
    block_send,
    block_recv,
    z_send,
    z_recv,
    zs_send,
    zs_recv,
    att_send,
    att_recv,
    c_send,
    c_recv,
    g_send,
    g_recv,
    d_send,
    d_recv,
    p_send,
    p_recv,
    act_send,
    act_recv,
    r_send,
    r_recv,
    f_send,
    f_recv,
):
    nz, ng, ne, grid, seqs, masked, group, cw, hw = dims
    ctx, e = lax.axis_index("ctx"), lax.axis_index("exp")
    z, core = ctx // 2, ctx % 2
    pair = 2 * z + 1 - core
    rows = seqs * masked
    span = seqs // PARTS
    pr = rows // PARTS
    steps = PARTS * ng
    slots = ne * SLOTS
    mine = blk(core, cw)
    factor = HD**-0.5 * math.log2(math.e)
    ny = grid[1]
    ex, ey = e // ny, e % ny
    peers = []
    for t in range(1, ne):
        peers.append(((ex + t // ny) % grid[0]) * ny + (ey + t % ny) % ny)

    def place_of(k):
        return k // ng, (z // 2 + ng // 2 + k % ng) % ng

    def piece(ref, p, half):
        return ref.at[half, blk(p, span)]

    def part_load(p):
        copies = [pltpu.make_async_copy(q_hbm.at[blk(p, pr)], q.at[blk(p, pr)], q_load.at[p])]
        for half in range(2):
            copies.append(
                pltpu.make_async_copy(
                    piece(cache_hbm, p, half), piece(kv, p, half), kv_load.at[p, half]
                )
            )
        return copies

    for p in range(PARTS):
        for copy in part_load(p):
            copy.start()

    barrier = pltpu.get_barrier_semaphore()
    pl.semaphore_signal(barrier, inc=1, device_id={"ctx": pair}, device_id_type=MESH)
    for t in range(1, nz):
        there = 2 * ((z + t) % nz) + core
        pl.semaphore_signal(barrier, inc=1, device_id={"ctx": there}, device_id_type=MESH)
    for peer in peers:
        pl.semaphore_signal(barrier, inc=1, device_id={"exp": peer}, device_id_type=MESH)

    block_rows = block_ref.shape[2]
    block[:, :, pl.ds(0, 16)] = jnp.zeros((2, seqs, 16, block.shape[3]), BF16)
    block[:, :, pl.ds(32, 96)] = jnp.zeros((2, seqs, 96, block.shape[3]), BF16)
    for s in range(seqs):
        for half in range(2):
            block[half, s, pl.ds(0, block_rows), :] = block_ref[half, s]

    pl.semaphore_wait(barrier, nz + ne - 1)

    block_mine = block.at[:, :, pl.ds(0, 16)]
    remote(
        block_mine, block.at[:, :, pl.ds(16, 16)], block_send, block_recv, ctx=pair
    ).start()

    for p in range(PARTS):
        for half in range(2):
            remote(
                piece(cache_hbm, p, half),
                piece(kv_pair, p, half),
                kv_send.at[p, half],
                kv_recv.at[p, half],
                ctx=pair,
            ).start()
    load_sin = pltpu.make_async_copy(stream_hbm.at[:, blk(ctx, cw)], sin, sin_load)
    load_sin.start()
    for b in range(nz):
        pltpu.make_async_copy(
            proj_hbm.at[:, blk(2 * b + core, cw)], wo.at[b, blk(core, 2 * HD)], wo_load
        ).start()
    for b in range(nz):
        remote(
            proj_hbm.at[:, blk(2 * b + 1 - core, cw)],
            wo.at[b, blk(core, 2 * HD)],
            wo_send,
            wo_recv,
            ctx=pair,
        ).start()

    lane = lax.broadcasted_iota(jnp.int32, (masked, 128), 1)
    block_lane = lax.broadcasted_iota(jnp.int32, (group // 2 * masked, 128), 1)
    block_live = (block_lane < 32) & (block_lane % 16 < block_rows)
    ones_keys = jnp.ones((kv.shape[2], HD), BF16)
    ones_block = jnp.ones((128, HD), BF16)
    wait_for(block_mine, block_recv)

    def attend(k, carry):
        p, j = place_of(k)

        @pl.when(k % ng == 0)
        def _():
            for copy in part_load(p):
                copy.wait()
            for half in range(2):
                wait_for(piece(kv_pair, p, half), kv_recv.at[p, half])

        for n in range(span):
            s = p * span + n
            here = blk(s, masked)
            local = pl.ds(n * masked, masked)
            column = blk(j, HD)
            heads = [j * group + (m // 2) * 4 + 2 * core + m % 2 for m in range(4)]
            qs = jnp.concatenate([q[here, blk(h, HD)] for h in heads], axis=0)
            scores = [
                dot_t(qs, kv[0, s, :, column]),
                dot_t(qs, kv_pair[0, s, :, column]),
                jnp.where(block_live, dot_t(qs, block[0, s, :, column]), -1e30),
            ]
            widest = scores[2]
            for m in range(kv.shape[2] // 128):
                cut = slice(m * 128, (m + 1) * 128)
                widest = jnp.maximum(widest, jnp.maximum(scores[0][:, cut], scores[1][:, cut]))
            peak = jnp.max(widest, axis=1, keepdims=True)
            weights = [jnp.exp2((part - peak) * factor).astype(BF16) for part in scores]
            both = dot(weights[0], jnp.concatenate([kv[1, s, :, column], ones_keys], axis=1))
            both += dot(
                weights[1], jnp.concatenate([kv_pair[1, s, :, column], ones_keys], axis=1)
            )
            both += dot(weights[2], jnp.concatenate([block[1, s, :, column], ones_block], axis=1))
            summed, total = both[:, :HD].astype(BF16), both[:, HD:]
            peak = peak * factor
            stats = jnp.zeros((masked, 128), F32)
            for m in range(4):
                zz, h = m // 2, m % 2
                cut = slice(m * masked, (m + 1) * masked)
                stats = jnp.where(lane == zz * 8 + h, peak[cut], stats)
                stats = jnp.where(lane == zz * 8 + h + 2, total[cut], stats)
                z_out[p, 2 * j + zz, local, pl.ds(h * HD, HD)] = summed[cut]
            stat[local, :] = stats
        turned = stat[...].T
        for zz in range(2):
            there = 2 * j + zz
            zs_out[p, there] = turned[zz * 8 : zz * 8 + 8]

            @pl.when(there == z)
            def _():
                z_in[p, there] = z_out[p, there]
                zs_in[p, there] = zs_out[p, there]

            @pl.when(there != z)
            def _():
                remote(
                    z_out.at[p, there],
                    z_in.at[p, z],
                    z_send.at[p, there],
                    z_recv.at[p, z],
                    ctx=2 * there + core,
                ).start()
                remote(
                    zs_out.at[p, there],
                    zs_in.at[p, z],
                    zs_send.at[p, there],
                    zs_recv.at[p, z],
                    ctx=2 * there + core,
                ).start()

        return carry

    stat[...] = jnp.zeros_like(stat)
    lax.fori_loop(0, steps, attend, 0)
    for half in range(2):
        pltpu.make_async_copy(
            in_hbm.at[half, 0], w_in.at[:, pl.ds(half * hw, hw)], in_load.at[half]
        ).start()
    for b in range(nz):
        pltpu.make_async_copy(
            down_hbm.at[0, :, blk(2 * b + core, cw)], wd.at[b, blk(core, hw)], wd_load
        ).start()


    def finish_heads(p):
        for t in range(1, nz):
            source = (z + t) % nz
            wait_for(z_in.at[p, source], z_recv.at[p, source])
            wait_for(zs_in.at[p, source], zs_recv.at[p, source])
        here = pl.ds(p * pr, pr)
        peaks = [zs_in[p, b, pl.ds(0, 2), :] for b in range(nz)]
        peak = functools.reduce(jnp.maximum, peaks)
        factors = [jnp.exp2(one - peak) for one in peaks]
        total = jnp.zeros((2, 128), F32)
        for b in range(nz):
            total = total + zs_in[p, b, pl.ds(2, 2), :] * factors[b]
        for b in range(nz):
            zs_in[p, b, pl.ds(4, 2), :] = factors[b] / total
        turned = jnp.concatenate([zs_in[p, b] for b in range(nz)], axis=0).T
        for h in range(2):
            summed = jnp.zeros((pr, HD), F32)
            for b in range(nz):
                f = turned[:pr, 8 * b + h + 4 : 8 * b + h + 5]
                summed = summed + z_in[p, b, :, pl.ds(h * HD, HD)].astype(F32) * f
            att[here, blk(2 * core + h, HD)] = summed.astype(BF16)
        return remote(
            att.at[here, mine], att.at[here, mine], att_send.at[p], att_recv.at[p], ctx=pair
        )

    def project(p):
        here = pl.ds(p * pr, pr)
        wait_for(att.at[here, mine], att_recv.at[p])
        heads = att[here, :]
        for t in range(1, nz):
            there = nearest(nz - t, z, nz)
            c_out[p, there] = dot(heads, wo[there]).astype(BF16)
            remote(
                c_out.at[p, there],
                c_in.at[p, z],
                c_send.at[p, there],
                c_recv.at[p, z],
                ctx=2 * there + core,
            ).start()

    def finish_stream(p):
        here = pl.ds(p * pr, pr)
        total = dot(att[here, :], wo[z]) + sin[here, :].astype(F32)
        for t in range(1, nz):
            source = nearest(t, z, nz)
            wait_for(c_in.at[p, source], c_recv.at[p, source])
            total = total + c_in[p, source].astype(F32)
        stream[here, :] = total.astype(BF16)
        for t in range(1, nz):
            there = nearest(t, z, nz)
            remote(
                stream.at[here],
                blocks.at[z, here],
                g_send.at[p, there],
                g_recv.at[p, z],
                ctx=2 * there + core,
            ).start()

    load_sin.wait()
    wait_for(wo.at[:, blk(core, 2 * HD)], wo_load)
    for p in range(PARTS):
        finish_heads(p).start()
        if p == 0:
            wait_for(wo.at[:, blk(core, 2 * HD)], wo_recv)
        project(p)

    for b in range(nz):
        remote(
            down_hbm.at[0, :, blk(2 * b + 1 - core, cw)],
            wd.at[b, blk(core, hw)],
            wd_send,
            wd_recv,
            ctx=pair,
        ).start()
    slot = lax.broadcasted_iota(jnp.int32, (slots, rows), 0)
    wanted = (slot // SLOTS) * nz + z
    hit = jnp.zeros((slots, rows), F32)
    weight = jnp.zeros((slots, rows), F32)
    ids, gates = ids_ref[...], gates_ref[...]
    for t in range(ids.shape[0]):
        same = ids[t : t + 1, :] == wanted
        hit = jnp.where(same, 1.0, hit)
        weight = jnp.where(same, gates[t : t + 1, :], weight)
    earlier = lax.broadcasted_iota(jnp.int32, (rows, rows), 0) < lax.broadcasted_iota(
        jnp.int32, (rows, rows), 1
    )
    rank = dot(hit.astype(BF16), earlier.astype(F32).astype(BF16))
    placed = jnp.where(rank == (slot % SLOTS).astype(F32), hit, 0.0)
    place[...] = placed.astype(BF16)
    combine[...] = (placed * weight).T.astype(BF16)
    squares[...] = jnp.zeros_like(squares)
    acc[...] = jnp.zeros_like(acc)

    for p in range(PARTS):
        finish_stream(p)
    blocks[z] = stream[...]

    def dispatch(t):
        b = nearest(t, z, nz)

        @pl.when(t > 0)
        def _():
            for p in range(PARTS):
                wait_for(blocks.at[b, pl.ds(p * pr, pr)], g_recv.at[p, b])

        d_out[b] = dot(place[...], blocks[b]).astype(BF16)
        for peer in peers:
            remote(
                d_out.at[b, blk(peer, SLOTS)],
                d_in.at[b, blk(e, SLOTS), mine],
                d_send.at[b],
                d_recv.at[b],
                exp=peer,
            ).start()
        d_in[b, blk(e, SLOTS), mine] = d_out[b, blk(e, SLOTS)]

    got = pl.ds(0, slots - SLOTS)

    def take(t):
        b = nearest(t, z, nz)
        wait_for(d_in.at[b, got, mine], d_recv.at[b])
        remote(
            d_in.at[b, :, mine], d_in.at[b, :, mine], p_send.at[b], p_recv.at[b], ctx=pair
        ).start()

    def feed(t):
        b = nearest(t, z, nz)
        wait_for(d_in.at[b, :, mine], p_recv.at[b])
        wide = d_in[b].astype(F32)
        squared = wide * wide
        part = squares[...]
        for n in range(2 * cw // 128):
            part = part + squared[:, n * 128 : (n + 1) * 128]
        squares[...] = part
        scaled = (wide * gain_ref[:, blk(b, 2 * cw)]).astype(BF16)
        acc[...] = acc[...] + dot(scaled, w_in[blk(b, 2 * cw), :])

    lag = nz // 2

    def lead(t, carry):
        dispatch(t)
        return carry

    lax.fori_loop(0, lag, lead, 0)
    for half in range(2):
        pltpu.make_async_copy(
            in_hbm.at[half, 0], w_in.at[:, pl.ds(half * hw, hw)], in_load.at[half]
        ).wait()

    def turn_in(t, carry):
        @pl.when(t < nz)
        def _():
            dispatch(t)

        @pl.when(t < nz + lag)
        def _():
            take(t - lag)

        @pl.when(t > lag)
        def _():
            feed(t - lag - 1)

        return carry

    lax.fori_loop(lag, nz + lag + 1, turn_in, 0)

    mean = jnp.sum(squares[...], axis=1, keepdims=True) * (1.0 / (2 * nz * cw))
    inverse = lax.rsqrt(mean + 1e-6)
    gate = acc[:, pl.ds(0, hw)] * inverse
    up = acc[:, pl.ds(hw, hw)] * inverse
    act_mine = act.at[:, blk(core, hw)]
    act[:, blk(core, hw)] = (gate / (1.0 + jnp.exp(-gate)) * up).astype(BF16)
    remote(act_mine, act_mine, act_send, act_recv, ctx=pair).start()
    wait_for(wd.at[:, blk(core, hw)], wd_load)
    wait_for(wd.at[:, blk(core, hw)], wd_recv)
    wait_for(act_mine, act_recv)

    def give(t):
        b = nearest(nz - 1 - t, z, nz)
        r_out[b] = dot(act[...], wd[b]).astype(BF16)
        for peer in peers:
            remote(
                r_out.at[b, blk(peer, SLOTS)],
                r_in.at[b, blk(e, SLOTS)],
                r_send.at[b],
                r_recv.at[b],
                exp=peer,
            ).start()
        r_in[b, blk(e, SLOTS)] = r_out[b, blk(e, SLOTS)]

    def join(t):
        b = nearest(nz - 1 - t, z, nz)
        wait_for(r_in.at[b, got], r_recv.at[b])
        f_out[b] = dot(combine[...], r_in[b]).astype(BF16)

        @pl.when(b != z)
        def _():
            remote(
                f_out.at[b], f_in.at[z], f_send.at[b], f_recv.at[z], ctx=2 * b + core
            ).start()

    def lead_back(t, carry):
        give(t)
        return carry

    lax.fori_loop(0, lag, lead_back, 0)

    def turn_back(t, carry):
        @pl.when(t < nz)
        def _():
            give(t)

        join(t - lag)
        return carry

    lax.fori_loop(lag, nz + lag, turn_back, 0)

    total = f_out[z].astype(F32)
    for t in range(1, nz):
        source = nearest(t, z, nz)
        wait_for(f_in.at[source], f_recv.at[source])
        total = total + f_in[source].astype(F32)
    out_ref[...] = (stream[...].astype(F32) + total).astype(BF16)

    wait_for(wo.at[:, blk(core, 2 * HD)], wo_send)
    wait_for(wd.at[:, blk(core, hw)], wd_send)
    wait_for(act_mine, act_send)

    for p in range(PARTS):
        for half in range(2):
            wait_for(piece(kv, p, half), kv_send.at[p, half])
    wait_for(block_mine, block_send)

    def drain_block(b, carry):
        wait_for(d_out.at[b, got], d_send.at[b])
        wait_for(r_out.at[b, got], r_send.at[b])
        wait_for(d_in.at[b, :, mine], p_send.at[b])
        return carry

    lax.fori_loop(0, nz, drain_block, 0)

    def drain_z(t, carry):
        there = (z + t) % nz
        wait_for(f_out.at[there], f_send.at[there])
        for p in range(PARTS):
            here = pl.ds(p * pr, pr)
            wait_for(z_out.at[p, there], z_send.at[p, there])
            wait_for(zs_out.at[p, there], zs_send.at[p, there])
            wait_for(c_out.at[p, there], c_send.at[p, there])
            wait_for(stream.at[here], g_send.at[p, there])
        return carry

    lax.fori_loop(1, nz, drain_z, 0)
    for p in range(PARTS):
        wait_for(att.at[pl.ds(p * pr, pr), mine], att_send.at[p])


def body(
    queries,
    cache_kv,
    block_kv,
    stream_in,
    out_proj,
    norm_gain,
    expert_ids,
    gate_weights,
    expert_in,
    expert_out,
):
    ctx_size, ne = lax.axis_size("ctx"), lax.axis_size("exp")
    nz = ctx_size // 2
    rows, width = queries.shape
    seqs = cache_kv.shape[1]
    masked = rows // seqs
    ng = cache_kv.shape[3] // HD
    group = width // HD // ng
    cw, hw = width // ctx_size, expert_in.shape[3]
    slots = ne * SLOTS
    grid = (4, 4) if ne == 16 else (1, ne)
    steps, pr = PARTS * ng, rows // PARTS
    dma, vm = pltpu.SemaphoreType.DMA, pltpu.VMEM
    anyspace = pl.BlockSpec(memory_space=pl.ANY)
    vmem = pl.BlockSpec(memory_space=pltpu.VMEM)
    dims = (nz, ng, ne, grid, seqs, masked, group, cw, hw)
    buffers = [
        vm((rows, width), BF16),
        vm(cache_kv.shape, BF16),
        vm(cache_kv.shape, BF16),
        vm((2, seqs, 128, cache_kv.shape[3]), BF16),
        vm((rows, cw), BF16),
        vm((nz, 4 * HD, cw), BF16),
        vm((width, 2 * hw), BF16),
        vm((nz, 2 * hw, cw), BF16),
        vm((128, 128), F32),
        vm((PARTS, nz, pr, 2 * HD), BF16),
        vm((PARTS, nz, pr, 2 * HD), BF16),
        vm((PARTS, nz, 8, 128), F32),
        vm((PARTS, nz, 8, 128), F32),
        vm((rows, 4 * HD), BF16),
        vm((PARTS, nz, pr, cw), BF16),
        vm((PARTS, nz, pr, cw), BF16),
        vm((rows, cw), BF16),
        vm((nz, rows, cw), BF16),
        vm((slots, rows), BF16),
        vm((rows, slots), BF16),
        vm((nz, slots, cw), BF16),
        vm((nz, slots, 2 * cw), BF16),
        vm((slots, 128), F32),
        vm((slots, 2 * hw), F32),
        vm((slots, 2 * hw), BF16),
        vm((nz, slots, cw), BF16),
        vm((nz, slots, cw), BF16),
        vm((nz, rows, cw), BF16),
        vm((nz, rows, cw), BF16),
    ]
    counts = [(PARTS,), (PARTS, 2)] + [()] * 4 + [(2,)] + [()] * 3
    counts += [(PARTS, 2)] * 2 + [()] * 2 + [(PARTS, nz)] * 4 + [(PARTS,)] * 2 + [(PARTS, nz)] * 4
    counts += [(nz,)] * 4 + [()] * 2 + [(nz,)] * 4
    return pl.pallas_call(
        functools.partial(layer_kernel, dims),
        out_shape=jax.ShapeDtypeStruct((rows, cw), BF16),
        in_specs=[anyspace, anyspace, vmem, anyspace, anyspace, vmem, vmem, vmem]
        + [anyspace, anyspace],
        out_specs=vmem,
        scratch_shapes=buffers + [dma(shape) for shape in counts],
        compiler_params=pltpu.CompilerParams(
            collective_id=1, has_side_effects=True, vmem_limit_bytes=VMEM_LIMIT
        ),
    )(
        queries,
        cache_kv,
        block_kv,
        stream_in,
        out_proj,
        norm_gain.reshape(1, width),
        expert_ids.T,
        gate_weights.T,
        expert_in,
        expert_out,
    )


def solution(mesh):
    placed = (
        P("exp", None),
        P(None, "exp", "ctx", None),
        P(None, "exp", "ctx", None),
        P("exp", None),
        P("ctx", None),
        P(),
        P("exp", None),
        P("exp", None),
        P(None, "exp", None, "ctx"),
        P("exp", "ctx", None),
    )
    return jax.shard_map(
        body, mesh=mesh, in_specs=placed, out_specs=P("exp", "ctx"), check_vma=False
    )
```

```python
import functools
import math

import jax
import jax.numpy as jnp
from jax import lax
from jax.experimental import pallas as pl
from jax.experimental.pallas import tpu as pltpu
from jax.sharding import PartitionSpec as P

HD = 128
SLOTS = 16
PARTS = 2
MESH = pl.DeviceIdType.MESH
F32 = jnp.float32
BF16 = jnp.bfloat16
VMEM_LIMIT = 60 * 1024 * 1024


def dot(a, b):
    return jnp.dot(a, b, preferred_element_type=F32)


def dot_t(a, b):
    return lax.dot_general(a, b, (((1,), (1,)), ((), ())), preferred_element_type=F32)


def remote(src, dst, send_sem, recv_sem, **where):
    return pltpu.make_async_remote_copy(
        src_ref=src,
        dst_ref=dst,
        send_sem=send_sem,
        recv_sem=recv_sem,
        device_id=where,
        device_id_type=MESH,
    )


def wait_for(ref, sem):
    pltpu.make_async_copy(ref, ref, sem).wait()


def blk(index, size):
    return pl.ds(pl.multiple_of(index * size, size), size)


def nearest(step, here, count):
    odd = step % 2
    return (here + odd * ((step + 1) // 2) + (1 - odd) * (count - step // 2)) % count


def layer_kernel(
    dims,
    q_hbm,
    cache_hbm,
    block_ref,
    stream_hbm,
    proj_hbm,
    gain_ref,
    ids_ref,
    gates_ref,
    in_hbm,
    down_hbm,
    out_ref,
    q,
    kv,
    kv_pair,
    block,
    sin,
    wo,
    w_in,
    wd,
    stat,
    z_out,
    z_in,
    zs_out,
    zs_in,
    att,
    c_out,
    c_in,
    stream,
    blocks,
    place,
    combine,
    d_out,
    d_in,
    squares,
    acc,
    act,
    r_out,
    r_in,
    f_out,
    f_in,
    q_load,
    kv_load,
    sin_load,
    wo_load,
    wo_send,
    wo_recv,
    in_load,
    wd_load,
    wd_send,
    wd_recv,
    kv_send,
    kv_recv,
    block_send,
    block_recv,
    z_send,
    z_recv,
    zs_send,
    zs_recv,
    att_send,
    att_recv,
    c_send,
    c_recv,
    g_send,
    g_recv,
    h_send,
    d_send,
    d_recv,
    p_send,
    p_recv,
    act_send,
    act_recv,
    r_send,
    r_recv,
    f_send,
    f_recv,
):
    nz, ng, ne, grid, seqs, masked, group, cw, hw = dims
    ctx, e = lax.axis_index("ctx"), lax.axis_index("exp")
    z, core = ctx // 2, ctx % 2
    pair = 2 * z + 1 - core
    rows = seqs * masked
    span = seqs // PARTS
    pr = rows // PARTS
    steps = PARTS * ng
    slots = ne * SLOTS
    mine = blk(core, cw)
    factor = HD**-0.5 * math.log2(math.e)
    ny = grid[1]
    ex, ey = e // ny, e % ny
    peers = []
    steps_away = [min(t // ny, grid[0] - t // ny) + min(t % ny, ny - t % ny) for t in range(ne)]
    for t in sorted(range(1, ne), key=lambda t: -steps_away[t]):
        peers.append(((ex + t // ny) % grid[0]) * ny + (ey + t % ny) % ny)

    def place_of(k):
        return k // ng, (z // 2 + ng // 2 + k % ng) % ng

    def piece(ref, p, half):
        return ref.at[half, blk(p, span)]

    def part_load(p):
        copies = [pltpu.make_async_copy(q_hbm.at[blk(p, pr)], q.at[blk(p, pr)], q_load.at[p])]
        for half in range(2):
            copies.append(
                pltpu.make_async_copy(
                    piece(cache_hbm, p, half), piece(kv, p, half), kv_load.at[p, half]
                )
            )
        return copies

    for p in range(PARTS):
        for copy in part_load(p):
            copy.start()

    barrier = pltpu.get_barrier_semaphore()
    pl.semaphore_signal(barrier, inc=1, device_id={"ctx": pair}, device_id_type=MESH)
    for t in range(1, nz):
        there = 2 * ((z + t) % nz) + core
        pl.semaphore_signal(barrier, inc=1, device_id={"ctx": there}, device_id_type=MESH)
    for peer in peers:
        pl.semaphore_signal(barrier, inc=1, device_id={"exp": peer}, device_id_type=MESH)

    block_rows = block_ref.shape[2]
    block[:, :, pl.ds(0, 16)] = jnp.zeros((2, seqs, 16, block.shape[3]), BF16)
    block[:, :, pl.ds(32, 96)] = jnp.zeros((2, seqs, 96, block.shape[3]), BF16)
    for s in range(seqs):
        for half in range(2):
            block[half, s, pl.ds(0, block_rows), :] = block_ref[half, s]

    pl.semaphore_wait(barrier, nz + ne - 1)

    block_mine = block.at[:, :, pl.ds(0, 16)]
    remote(
        block_mine, block.at[:, :, pl.ds(16, 16)], block_send, block_recv, ctx=pair
    ).start()

    for p in range(PARTS):
        for half in range(2):
            remote(
                piece(cache_hbm, p, half),
                piece(kv_pair, p, half),
                kv_send.at[p, half],
                kv_recv.at[p, half],
                ctx=pair,
            ).start()
    load_sin = pltpu.make_async_copy(stream_hbm.at[:, blk(ctx, cw)], sin, sin_load)
    load_sin.start()
    for b in range(nz):
        pltpu.make_async_copy(
            proj_hbm.at[:, blk(2 * b + core, cw)], wo.at[b, blk(core, 2 * HD)], wo_load
        ).start()
    for b in range(nz):
        remote(
            proj_hbm.at[:, blk(2 * b + 1 - core, cw)],
            wo.at[b, blk(core, 2 * HD)],
            wo_send,
            wo_recv,
            ctx=pair,
        ).start()

    lane = lax.broadcasted_iota(jnp.int32, (masked, 128), 1)
    block_lane = lax.broadcasted_iota(jnp.int32, (group // 2 * masked, 128), 1)
    block_live = (block_lane < 32) & (block_lane % 16 < block_rows)
    ones_keys = jnp.ones((kv.shape[2], HD), BF16)
    ones_block = jnp.ones((128, HD), BF16)
    wait_for(block_mine, block_recv)

    def attend(k, carry):
        p, j = place_of(k)

        @pl.when(k % ng == 0)
        def _():
            for copy in part_load(p):
                copy.wait()
            for half in range(2):
                wait_for(piece(kv_pair, p, half), kv_recv.at[p, half])

        for n in range(span):
            s = p * span + n
            here = blk(s, masked)
            local = pl.ds(n * masked, masked)
            column = blk(j, HD)
            heads = [j * group + (m // 2) * 4 + 2 * core + m % 2 for m in range(4)]
            qs = jnp.concatenate([q[here, blk(h, HD)] for h in heads], axis=0)
            scores = [
                dot_t(qs, kv[0, s, :, column]),
                dot_t(qs, kv_pair[0, s, :, column]),
                jnp.where(block_live, dot_t(qs, block[0, s, :, column]), -1e30),
            ]
            widest = scores[2]
            for m in range(kv.shape[2] // 128):
                cut = slice(m * 128, (m + 1) * 128)
                widest = jnp.maximum(widest, jnp.maximum(scores[0][:, cut], scores[1][:, cut]))
            peak = jnp.max(widest, axis=1, keepdims=True)
            weights = [jnp.exp2((part - peak) * factor).astype(BF16) for part in scores]
            both = dot(weights[0], jnp.concatenate([kv[1, s, :, column], ones_keys], axis=1))
            both += dot(
                weights[1], jnp.concatenate([kv_pair[1, s, :, column], ones_keys], axis=1)
            )
            both += dot(weights[2], jnp.concatenate([block[1, s, :, column], ones_block], axis=1))
            summed, total = both[:, :HD].astype(BF16), both[:, HD:]
            peak = peak * factor
            stats = jnp.zeros((masked, 128), F32)
            for m in range(4):
                zz, h = m // 2, m % 2
                cut = slice(m * masked, (m + 1) * masked)
                stats = jnp.where(lane == zz * 8 + h, peak[cut], stats)
                stats = jnp.where(lane == zz * 8 + h + 2, total[cut], stats)
                z_out[p, 2 * j + zz, local, pl.ds(h * HD, HD)] = summed[cut]
            stat[local, :] = stats
        turned = stat[...].T
        for zz in range(2):
            there = 2 * j + zz
            zs_out[p, there] = turned[zz * 8 : zz * 8 + 8]

            @pl.when(there == z)
            def _():
                z_in[p, there] = z_out[p, there]
                zs_in[p, there] = zs_out[p, there]

            @pl.when(there != z)
            def _():
                remote(
                    z_out.at[p, there],
                    z_in.at[p, z],
                    z_send.at[p, there],
                    z_recv.at[p, z],
                    ctx=2 * there + core,
                ).start()
                remote(
                    zs_out.at[p, there],
                    zs_in.at[p, z],
                    zs_send.at[p, there],
                    zs_recv.at[p, z],
                    ctx=2 * there + core,
                ).start()

        return carry

    stat[...] = jnp.zeros_like(stat)
    lax.fori_loop(0, steps, attend, 0)
    for half in range(2):
        pltpu.make_async_copy(
            in_hbm.at[half, 0], w_in.at[:, pl.ds(half * hw, hw)], in_load.at[half]
        ).start()
    for b in range(nz):
        pltpu.make_async_copy(
            down_hbm.at[0, :, blk(2 * b + core, cw)], wd.at[b, blk(core, hw)], wd_load
        ).start()


    def finish_heads(p):
        for t in range(1, nz):
            source = (z + t) % nz
            wait_for(z_in.at[p, source], z_recv.at[p, source])
            wait_for(zs_in.at[p, source], zs_recv.at[p, source])
        here = pl.ds(p * pr, pr)
        peaks = [zs_in[p, b, pl.ds(0, 2), :] for b in range(nz)]
        peak = functools.reduce(jnp.maximum, peaks)
        factors = [jnp.exp2(one - peak) for one in peaks]
        total = jnp.zeros((2, 128), F32)
        for b in range(nz):
            total = total + zs_in[p, b, pl.ds(2, 2), :] * factors[b]
        for b in range(nz):
            zs_in[p, b, pl.ds(4, 2), :] = factors[b] / total
        turned = jnp.concatenate([zs_in[p, b] for b in range(nz)], axis=0).T
        for h in range(2):
            summed = jnp.zeros((pr, HD), F32)
            for b in range(nz):
                f = turned[:pr, 8 * b + h + 4 : 8 * b + h + 5]
                summed = summed + z_in[p, b, :, pl.ds(h * HD, HD)].astype(F32) * f
            att[here, blk(2 * core + h, HD)] = summed.astype(BF16)
        return remote(
            att.at[here, mine], att.at[here, mine], att_send.at[p], att_recv.at[p], ctx=pair
        )

    def project(p):
        here = pl.ds(p * pr, pr)
        wait_for(att.at[here, mine], att_recv.at[p])
        heads = att[here, :]
        for t in range(1, nz):
            there = nearest(nz - t, z, nz)
            c_out[p, there] = dot(heads, wo[there]).astype(BF16)
            remote(
                c_out.at[p, there],
                c_in.at[p, z],
                c_send.at[p, there],
                c_recv.at[p, z],
                ctx=2 * there + core,
            ).start()

    def finish_stream(p):
        here = pl.ds(p * pr, pr)
        total = dot(att[here, :], wo[z]) + sin[here, :].astype(F32)
        for t in range(1, nz):
            source = nearest(t, z, nz)
            wait_for(c_in.at[p, source], c_recv.at[p, source])
            total = total + c_in[p, source].astype(F32)
        stream[here, :] = total.astype(BF16)
        for t in range(1, min(nz, 5)):
            there = nearest(t, z, nz)
            remote(
                stream.at[here],
                blocks.at[z, here],
                g_send.at[p, there],
                g_recv.at[p, z],
                ctx=2 * there + core,
            ).start()

    def hand_on(b, first, second):
        for p in range(PARTS):
            here = pl.ds(p * pr, pr)
            there = (z + first) % nz
            remote(
                blocks.at[b, here],
                blocks.at[b, here],
                h_send.at[p, there],
                g_recv.at[p, b],
                ctx=2 * there + core,
            ).start()
        here = pl.ds((first == 1) * pr, pr)
        there = (z + second) % nz
        part = int(first == 1)
        remote(
            blocks.at[b, here],
            blocks.at[b, here],
            h_send.at[part, there],
            g_recv.at[part, b],
            ctx=2 * there + core,
        ).start()

    load_sin.wait()
    wait_for(wo.at[:, blk(core, 2 * HD)], wo_load)
    for p in range(PARTS):
        finish_heads(p).start()
        if p == 0:
            wait_for(wo.at[:, blk(core, 2 * HD)], wo_recv)
        project(p)

    for b in range(nz):
        remote(
            down_hbm.at[0, :, blk(2 * b + 1 - core, cw)],
            wd.at[b, blk(core, hw)],
            wd_send,
            wd_recv,
            ctx=pair,
        ).start()
    slot = lax.broadcasted_iota(jnp.int32, (slots, rows), 0)
    wanted = (slot // SLOTS) * nz + z
    hit = jnp.zeros((slots, rows), F32)
    weight = jnp.zeros((slots, rows), F32)
    ids, gates = ids_ref[...], gates_ref[...]
    for t in range(ids.shape[0]):
        same = ids[t : t + 1, :] == wanted
        hit = jnp.where(same, 1.0, hit)
        weight = jnp.where(same, gates[t : t + 1, :], weight)
    earlier = lax.broadcasted_iota(jnp.int32, (rows, rows), 0) < lax.broadcasted_iota(
        jnp.int32, (rows, rows), 1
    )
    rank = dot(hit.astype(BF16), earlier.astype(F32).astype(BF16))
    placed = jnp.where(rank == (slot % SLOTS).astype(F32), hit, 0.0)
    place[...] = placed.astype(BF16)
    combine[...] = (placed * weight).T.astype(BF16)
    squares[...] = jnp.zeros_like(squares)
    acc[...] = jnp.zeros_like(acc)

    for p in range(PARTS):
        finish_stream(p)
    blocks[z] = stream[...]

    def dispatch(t):
        b = nearest(t, z, nz)

        @pl.when(t > 0)
        def _():
            for p in range(PARTS):
                wait_for(blocks.at[b, pl.ds(p * pr, pr)], g_recv.at[p, b])

        if nz == 8:

            @pl.when(t == 3)
            def _():
                hand_on(b, nz - 1, nz - 2)

            @pl.when(t == 4)
            def _():
                hand_on(b, 1, 2)

        d_out[b] = dot(place[...], blocks[b]).astype(BF16)
        for peer in peers:
            remote(
                d_out.at[b, blk(peer, SLOTS)],
                d_in.at[b, blk(e, SLOTS), mine],
                d_send.at[b],
                d_recv.at[b],
                exp=peer,
            ).start()
        d_in[b, blk(e, SLOTS), mine] = d_out[b, blk(e, SLOTS)]

    got = pl.ds(0, slots - SLOTS)

    def take(t):
        b = nearest(t, z, nz)
        wait_for(d_in.at[b, got, mine], d_recv.at[b])
        remote(
            d_in.at[b, :, mine], d_in.at[b, :, mine], p_send.at[b], p_recv.at[b], ctx=pair
        ).start()

    def feed(t):
        b = nearest(t, z, nz)
        wait_for(d_in.at[b, :, mine], p_recv.at[b])
        wide = d_in[b].astype(F32)
        squared = wide * wide
        part = squares[...]
        for n in range(2 * cw // 128):
            part = part + squared[:, n * 128 : (n + 1) * 128]
        squares[...] = part
        scaled = (wide * gain_ref[:, blk(b, 2 * cw)]).astype(BF16)
        acc[...] = acc[...] + dot(scaled, w_in[blk(b, 2 * cw), :])

    lag = nz // 2

    def lead(t, carry):
        dispatch(t)
        return carry

    lax.fori_loop(0, lag, lead, 0)
    for half in range(2):
        pltpu.make_async_copy(
            in_hbm.at[half, 0], w_in.at[:, pl.ds(half * hw, hw)], in_load.at[half]
        ).wait()

    def turn_in(t, carry):
        @pl.when(t < nz)
        def _():
            dispatch(t)

        @pl.when(t < nz + lag)
        def _():
            take(t - lag)

        @pl.when(t > lag)
        def _():
            feed(t - lag - 1)

        return carry

    lax.fori_loop(lag, nz + lag + 1, turn_in, 0)

    mean = jnp.sum(squares[...], axis=1, keepdims=True) * (1.0 / (2 * nz * cw))
    inverse = lax.rsqrt(mean + 1e-6)
    gate = acc[:, pl.ds(0, hw)] * inverse
    up = acc[:, pl.ds(hw, hw)] * inverse
    act_mine = act.at[:, blk(core, hw)]
    act[:, blk(core, hw)] = (gate / (1.0 + jnp.exp(-gate)) * up).astype(BF16)
    remote(act_mine, act_mine, act_send, act_recv, ctx=pair).start()
    wait_for(wd.at[:, blk(core, hw)], wd_load)
    wait_for(wd.at[:, blk(core, hw)], wd_recv)
    wait_for(act_mine, act_recv)

    def give(t):
        b = nearest(nz - 1 - t, z, nz)
        r_out[b] = dot(act[...], wd[b]).astype(BF16)
        for peer in peers:
            remote(
                r_out.at[b, blk(peer, SLOTS)],
                r_in.at[b, blk(e, SLOTS)],
                r_send.at[b],
                r_recv.at[b],
                exp=peer,
            ).start()
        r_in[b, blk(e, SLOTS)] = r_out[b, blk(e, SLOTS)]

    def join(t):
        b = nearest(nz - 1 - t, z, nz)
        wait_for(r_in.at[b, got], r_recv.at[b])
        f_out[b] = dot(combine[...], r_in[b]).astype(BF16)

        @pl.when(b != z)
        def _():
            remote(
                f_out.at[b], f_in.at[z], f_send.at[b], f_recv.at[z], ctx=2 * b + core
            ).start()

    def lead_back(t, carry):
        give(t)
        return carry

    lax.fori_loop(0, lag, lead_back, 0)

    def turn_back(t, carry):
        @pl.when(t < nz)
        def _():
            give(t)

        join(t - lag)
        return carry

    lax.fori_loop(lag, nz + lag, turn_back, 0)

    total = f_out[z].astype(F32)
    for t in range(1, nz):
        source = nearest(t, z, nz)
        wait_for(f_in.at[source], f_recv.at[source])
        total = total + f_in[source].astype(F32)
    out_ref[...] = (stream[...].astype(F32) + total).astype(BF16)

    wait_for(wo.at[:, blk(core, 2 * HD)], wo_send)
    wait_for(wd.at[:, blk(core, hw)], wd_send)
    wait_for(act_mine, act_send)

    for p in range(PARTS):
        for half in range(2):
            wait_for(piece(kv, p, half), kv_send.at[p, half])
    wait_for(block_mine, block_send)

    def drain_block(b, carry):
        wait_for(d_out.at[b, got], d_send.at[b])
        wait_for(r_out.at[b, got], r_send.at[b])
        wait_for(d_in.at[b, :, mine], p_send.at[b])
        return carry

    lax.fori_loop(0, nz, drain_block, 0)

    def drain_z(t, carry):
        there = (z + t) % nz
        wait_for(f_out.at[there], f_send.at[there])
        for p in range(PARTS):
            here = pl.ds(p * pr, pr)
            wait_for(z_out.at[p, there], z_send.at[p, there])
            wait_for(zs_out.at[p, there], zs_send.at[p, there])
            wait_for(c_out.at[p, there], c_send.at[p, there])
        return carry

    lax.fori_loop(1, nz, drain_z, 0)
    for p in range(PARTS):
        here = pl.ds(p * pr, pr)
        for t in range(1, min(nz, 5)):
            there = nearest(t, z, nz)
            wait_for(stream.at[here], g_send.at[p, there])
        if nz == 8:
            for t in (1, nz - 1, 2 if p == 1 else nz - 2):
                wait_for(stream.at[here], h_send.at[p, (z + t) % nz])
    for p in range(PARTS):
        wait_for(att.at[pl.ds(p * pr, pr), mine], att_send.at[p])


def body(
    queries,
    cache_kv,
    block_kv,
    stream_in,
    out_proj,
    norm_gain,
    expert_ids,
    gate_weights,
    expert_in,
    expert_out,
):
    ctx_size, ne = lax.axis_size("ctx"), lax.axis_size("exp")
    nz = ctx_size // 2
    rows, width = queries.shape
    seqs = cache_kv.shape[1]
    masked = rows // seqs
    ng = cache_kv.shape[3] // HD
    group = width // HD // ng
    cw, hw = width // ctx_size, expert_in.shape[3]
    slots = ne * SLOTS
    grid = (4, 4) if ne == 16 else (1, ne)
    steps, pr = PARTS * ng, rows // PARTS
    dma, vm = pltpu.SemaphoreType.DMA, pltpu.VMEM
    anyspace = pl.BlockSpec(memory_space=pl.ANY)
    vmem = pl.BlockSpec(memory_space=pltpu.VMEM)
    dims = (nz, ng, ne, grid, seqs, masked, group, cw, hw)
    buffers = [
        vm((rows, width), BF16),
        vm(cache_kv.shape, BF16),
        vm(cache_kv.shape, BF16),
        vm((2, seqs, 128, cache_kv.shape[3]), BF16),
        vm((rows, cw), BF16),
        vm((nz, 4 * HD, cw), BF16),
        vm((width, 2 * hw), BF16),
        vm((nz, 2 * hw, cw), BF16),
        vm((128, 128), F32),
        vm((PARTS, nz, pr, 2 * HD), BF16),
        vm((PARTS, nz, pr, 2 * HD), BF16),
        vm((PARTS, nz, 8, 128), F32),
        vm((PARTS, nz, 8, 128), F32),
        vm((rows, 4 * HD), BF16),
        vm((PARTS, nz, pr, cw), BF16),
        vm((PARTS, nz, pr, cw), BF16),
        vm((rows, cw), BF16),
        vm((nz, rows, cw), BF16),
        vm((slots, rows), BF16),
        vm((rows, slots), BF16),
        vm((nz, slots, cw), BF16),
        vm((nz, slots, 2 * cw), BF16),
        vm((slots, 128), F32),
        vm((slots, 2 * hw), F32),
        vm((slots, 2 * hw), BF16),
        vm((nz, slots, cw), BF16),
        vm((nz, slots, cw), BF16),
        vm((nz, rows, cw), BF16),
        vm((nz, rows, cw), BF16),
    ]
    counts = [(PARTS,), (PARTS, 2)] + [()] * 4 + [(2,)] + [()] * 3
    counts += [(PARTS, 2)] * 2 + [()] * 2 + [(PARTS, nz)] * 4 + [(PARTS,)] * 2 + [(PARTS, nz)] * 5
    counts += [(nz,)] * 4 + [()] * 2 + [(nz,)] * 4
    return pl.pallas_call(
        functools.partial(layer_kernel, dims),
        out_shape=jax.ShapeDtypeStruct((rows, cw), BF16),
        in_specs=[anyspace, anyspace, vmem, anyspace, anyspace, vmem, vmem, vmem]
        + [anyspace, anyspace],
        out_specs=vmem,
        scratch_shapes=buffers + [dma(shape) for shape in counts],
        compiler_params=pltpu.CompilerParams(
            collective_id=1, has_side_effects=True, vmem_limit_bytes=VMEM_LIMIT
        ),
    )(
        queries,
        cache_kv,
        block_kv,
        stream_in,
        out_proj,
        norm_gain.reshape(1, width),
        expert_ids.T,
        gate_weights.T,
        expert_in,
        expert_out,
    )


def solution(mesh):
    placed = (
        P("exp", None),
        P(None, "exp", "ctx", None),
        P(None, "exp", "ctx", None),
        P("exp", None),
        P("ctx", None),
        P(),
        P("exp", None),
        P("exp", None),
        P(None, "exp", None, "ctx"),
        P("exp", "ctx", None),
    )
    return jax.shard_map(
        body, mesh=mesh, in_specs=placed, out_specs=P("exp", "ctx"), check_vma=False
    )
```

```python
import functools
import math

import jax
import jax.numpy as jnp
from jax import lax
from jax.experimental import pallas as pl
from jax.experimental.pallas import tpu as pltpu
from jax.sharding import PartitionSpec as P

HD = 128
SLOTS = 16
PARTS = 2
MESH = pl.DeviceIdType.MESH
F32 = jnp.float32
BF16 = jnp.bfloat16
VMEM_LIMIT = 60 * 1024 * 1024


def dot(a, b):
    return jnp.dot(a, b, preferred_element_type=F32)


def dot_t(a, b):
    return lax.dot_general(a, b, (((1,), (1,)), ((), ())), preferred_element_type=F32)


def remote(src, dst, send_sem, recv_sem, **where):
    return pltpu.make_async_remote_copy(
        src_ref=src,
        dst_ref=dst,
        send_sem=send_sem,
        recv_sem=recv_sem,
        device_id=where,
        device_id_type=MESH,
    )


def wait_for(ref, sem):
    pltpu.make_async_copy(ref, ref, sem).wait()


def blk(index, size):
    return pl.ds(pl.multiple_of(index * size, size), size)


def nearest(step, here, count):
    odd = step % 2
    return (here + odd * ((step + 1) // 2) + (1 - odd) * (count - step // 2)) % count


def layer_kernel(
    dims,
    q_hbm,
    cache_hbm,
    block_hbm,
    stream_hbm,
    proj_hbm,
    gain_hbm,
    ids_hbm,
    gates_hbm,
    in_hbm,
    down_hbm,
    out_ref,
    q,
    kv,
    kv_pair,
    block_ref,
    gain_ref,
    ids_ref,
    gates_ref,
    block,
    sin,
    wo,
    w_in,
    wd,
    stat,
    z_out,
    z_in,
    zs_out,
    zs_in,
    att,
    c_out,
    c_in,
    stream,
    blocks,
    place,
    combine,
    d_out,
    d_in,
    squares,
    acc,
    act,
    r_out,
    r_in,
    f_out,
    f_in,
    small_load,
    q_load,
    kv_load,
    sin_load,
    wo_load,
    wo_send,
    wo_recv,
    in_load,
    wd_load,
    wd_send,
    wd_recv,
    kv_send,
    kv_recv,
    block_send,
    block_recv,
    z_send,
    z_recv,
    zs_send,
    zs_recv,
    att_send,
    att_recv,
    c_send,
    c_recv,
    g_send,
    g_recv,
    h_send,
    d_send,
    d_recv,
    p_send,
    p_recv,
    act_send,
    act_recv,
    r_send,
    r_recv,
    f_send,
    f_recv,
):
    nz, ng, ne, grid, seqs, masked, group, cw, hw = dims
    ctx, e = lax.axis_index("ctx"), lax.axis_index("exp")
    z, core = ctx // 2, ctx % 2
    pair = 2 * z + 1 - core
    rows = seqs * masked
    span = seqs // PARTS
    pr = rows // PARTS
    steps = PARTS * ng
    slots = ne * SLOTS
    mine = blk(core, cw)
    factor = HD**-0.5 * math.log2(math.e)
    ny = grid[1]
    ex, ey = e // ny, e % ny
    peers = []
    steps_away = [min(t // ny, grid[0] - t // ny) + min(t % ny, ny - t % ny) for t in range(ne)]
    for t in sorted(range(1, ne), key=lambda t: -steps_away[t]):
        peers.append(((ex + t // ny) % grid[0]) * ny + (ey + t % ny) % ny)

    def place_of(k):
        return k // ng, (z // 2 + ng // 2 + k % ng) % ng

    def piece(ref, p, half):
        return ref.at[half, blk(p, span)]

    def part_load(p):
        copies = [pltpu.make_async_copy(q_hbm.at[blk(p, pr)], q.at[blk(p, pr)], q_load.at[p])]
        for half in range(2):
            copies.append(
                pltpu.make_async_copy(
                    piece(cache_hbm, p, half), piece(kv, p, half), kv_load.at[p, half]
                )
            )
        return copies

    barrier = pltpu.get_barrier_semaphore()
    pl.semaphore_signal(barrier, inc=1, device_id={"ctx": pair}, device_id_type=MESH)
    for copy in part_load(0):
        copy.start()
    for t in range(1, nz):
        there = 2 * ((z + t) % nz) + core
        pl.semaphore_signal(barrier, inc=1, device_id={"ctx": there}, device_id_type=MESH)
    for peer in peers:
        pl.semaphore_signal(barrier, inc=1, device_id={"exp": peer}, device_id_type=MESH)

    for p in range(1, PARTS):
        for copy in part_load(p):
            copy.start()
    small = [
        pltpu.make_async_copy(source, here, small_load.at[n])
        for n, (source, here) in enumerate(
            [
                (block_hbm, block_ref),
                (gain_hbm, gain_ref),
                (ids_hbm, ids_ref),
                (gates_hbm, gates_ref),
            ]
        )
    ]
    for copy in small:
        copy.start()

    pl.semaphore_wait(barrier, nz + ne - 1)

    for p in range(PARTS):
        for half in range(2):
            remote(
                piece(cache_hbm, p, half),
                piece(kv_pair, p, half),
                kv_send.at[p, half],
                kv_recv.at[p, half],
                ctx=pair,
            ).start()
    block_rows = block_ref.shape[2]
    small[0].wait()
    block[:, :, pl.ds(0, 16)] = jnp.zeros((2, seqs, 16, block.shape[3]), BF16)
    block[:, :, pl.ds(32, 96)] = jnp.zeros((2, seqs, 96, block.shape[3]), BF16)
    for s in range(seqs):
        for half in range(2):
            block[half, s, pl.ds(0, block_rows), :] = block_ref[half, s]

    block_mine = block.at[:, :, pl.ds(0, 16)]
    remote(
        block_mine, block.at[:, :, pl.ds(16, 16)], block_send, block_recv, ctx=pair
    ).start()

    load_sin = pltpu.make_async_copy(stream_hbm.at[:, blk(ctx, cw)], sin, sin_load)
    load_sin.start()
    for b in range(nz):
        pltpu.make_async_copy(
            proj_hbm.at[:, blk(2 * b + core, cw)], wo.at[b, blk(core, 2 * HD)], wo_load
        ).start()
    for b in range(nz):
        remote(
            proj_hbm.at[:, blk(2 * b + 1 - core, cw)],
            wo.at[b, blk(core, 2 * HD)],
            wo_send,
            wo_recv,
            ctx=pair,
        ).start()

    lane = lax.broadcasted_iota(jnp.int32, (masked, 128), 1)
    block_lane = lax.broadcasted_iota(jnp.int32, (group // 2 * masked, 128), 1)
    block_live = (block_lane < 32) & (block_lane % 16 < block_rows)
    ones_keys = jnp.ones((kv.shape[2], HD), BF16)
    ones_block = jnp.ones((128, HD), BF16)
    wait_for(block_mine, block_recv)

    def await_keys(p):
        for copy in part_load(p)[:2]:
            copy.wait()
        wait_for(piece(kv_pair, p, 0), kv_recv.at[p, 0])

    def await_values(p):
        part_load(p)[2].wait()
        wait_for(piece(kv_pair, p, 1), kv_recv.at[p, 1])

    def attend(k, first):
        p, j = place_of(k)
        if first:
            await_keys(0)
        else:

            @pl.when(k % ng == 0)
            def _():
                await_keys(p)
                await_values(p)

        column = blk(j, HD)
        heads = [j * group + (m // 2) * 4 + 2 * core + m % 2 for m in range(4)]
        which = [p * span + n for n in range(span)]
        scores = []
        for s in which:
            qs = jnp.concatenate([q[blk(s, masked), blk(h, HD)] for h in heads], axis=0)
            scores.append(
                [
                    dot_t(qs, kv[0, s, :, column]),
                    dot_t(qs, kv_pair[0, s, :, column]),
                    jnp.where(block_live, dot_t(qs, block[0, s, :, column]), -1e30),
                ]
            )
        peaks = []
        for own, other, extra in scores:
            widest = extra
            for m in range(kv.shape[2] // 128):
                cut = slice(m * 128, (m + 1) * 128)
                widest = jnp.maximum(widest, jnp.maximum(own[:, cut], other[:, cut]))
            peaks.append(jnp.max(widest, axis=1, keepdims=True))
        weights = [
            [jnp.exp2((part - peak) * factor).astype(BF16) for part in parts]
            for parts, peak in zip(scores, peaks)
        ]
        if first:
            await_values(0)
        for n, s in enumerate(which):
            local = pl.ds(n * masked, masked)
            both = dot(weights[n][0], jnp.concatenate([kv[1, s, :, column], ones_keys], axis=1))
            both += dot(
                weights[n][1], jnp.concatenate([kv_pair[1, s, :, column], ones_keys], axis=1)
            )
            both += dot(
                weights[n][2], jnp.concatenate([block[1, s, :, column], ones_block], axis=1)
            )
            summed, total = both[:, :HD].astype(BF16), both[:, HD:]
            peak = peaks[n] * factor
            stats = jnp.zeros((masked, 128), F32)
            for m in range(4):
                zz, h = m // 2, m % 2
                cut = slice(m * masked, (m + 1) * masked)
                stats = jnp.where(lane == zz * 8 + h, peak[cut], stats)
                stats = jnp.where(lane == zz * 8 + h + 2, total[cut], stats)
                z_out[p, 2 * j + zz, local, pl.ds(h * HD, HD)] = summed[cut]
            stat[local, :] = stats
        turned = stat[...].T
        for zz in range(2):
            there = 2 * j + zz
            zs_out[p, there] = turned[zz * 8 : zz * 8 + 8]

            @pl.when(there == z)
            def _():
                z_in[p, there] = z_out[p, there]
                zs_in[p, there] = zs_out[p, there]

            @pl.when(there != z)
            def _():
                remote(
                    z_out.at[p, there],
                    z_in.at[p, z],
                    z_send.at[p, there],
                    z_recv.at[p, z],
                    ctx=2 * there + core,
                ).start()
                remote(
                    zs_out.at[p, there],
                    zs_in.at[p, z],
                    zs_send.at[p, there],
                    zs_recv.at[p, z],
                    ctx=2 * there + core,
                ).start()

    stat[...] = jnp.zeros_like(stat)
    attend(0, True)

    def turn(k, carry):
        attend(k, False)
        return carry

    lax.fori_loop(1, steps, turn, 0)
    for half in range(2):
        pltpu.make_async_copy(
            in_hbm.at[half, 0], w_in.at[:, pl.ds(half * hw, hw)], in_load.at[half]
        ).start()
    for b in range(nz):
        pltpu.make_async_copy(
            down_hbm.at[0, :, blk(2 * b + core, cw)], wd.at[b, blk(core, hw)], wd_load
        ).start()


    def finish_heads(p):
        for t in range(1, nz):
            source = (z + t) % nz
            wait_for(z_in.at[p, source], z_recv.at[p, source])
            wait_for(zs_in.at[p, source], zs_recv.at[p, source])
        here = pl.ds(p * pr, pr)
        peaks = [zs_in[p, b, pl.ds(0, 2), :] for b in range(nz)]
        peak = functools.reduce(jnp.maximum, peaks)
        factors = [jnp.exp2(one - peak) for one in peaks]
        total = jnp.zeros((2, 128), F32)
        for b in range(nz):
            total = total + zs_in[p, b, pl.ds(2, 2), :] * factors[b]
        for b in range(nz):
            zs_in[p, b, pl.ds(4, 2), :] = factors[b] / total
        turned = jnp.concatenate([zs_in[p, b] for b in range(nz)], axis=0).T
        for h in range(2):
            summed = jnp.zeros((pr, HD), F32)
            for b in range(nz):
                f = turned[:pr, 8 * b + h + 4 : 8 * b + h + 5]
                summed = summed + z_in[p, b, :, pl.ds(h * HD, HD)].astype(F32) * f
            att[here, blk(2 * core + h, HD)] = summed.astype(BF16)
        return remote(
            att.at[here, mine], att.at[here, mine], att_send.at[p], att_recv.at[p], ctx=pair
        )

    def project(p):
        here = pl.ds(p * pr, pr)
        wait_for(att.at[here, mine], att_recv.at[p])
        heads = att[here, :]
        for t in range(1, nz):
            there = nearest(nz - t, z, nz)
            c_out[p, there] = dot(heads, wo[there]).astype(BF16)
            remote(
                c_out.at[p, there],
                c_in.at[p, z],
                c_send.at[p, there],
                c_recv.at[p, z],
                ctx=2 * there + core,
            ).start()

    def finish_stream(p):
        here = pl.ds(p * pr, pr)
        total = dot(att[here, :], wo[z]) + sin[here, :].astype(F32)
        for t in range(1, nz):
            source = nearest(t, z, nz)
            wait_for(c_in.at[p, source], c_recv.at[p, source])
            total = total + c_in[p, source].astype(F32)
        stream[here, :] = total.astype(BF16)
        for t in range(1, min(nz, 5)):
            there = nearest(t, z, nz)
            remote(
                stream.at[here],
                blocks.at[z, here],
                g_send.at[p, there],
                g_recv.at[p, z],
                ctx=2 * there + core,
            ).start()

    def hand_on(b, first, second):
        for p in range(PARTS):
            here = pl.ds(p * pr, pr)
            there = (z + first) % nz
            remote(
                blocks.at[b, here],
                blocks.at[b, here],
                h_send.at[p, there],
                g_recv.at[p, b],
                ctx=2 * there + core,
            ).start()
        here = pl.ds((first == 1) * pr, pr)
        there = (z + second) % nz
        part = int(first == 1)
        remote(
            blocks.at[b, here],
            blocks.at[b, here],
            h_send.at[part, there],
            g_recv.at[part, b],
            ctx=2 * there + core,
        ).start()

    load_sin.wait()
    wait_for(wo.at[:, blk(core, 2 * HD)], wo_load)
    for p in range(PARTS):
        finish_heads(p).start()
        if p == 0:
            wait_for(wo.at[:, blk(core, 2 * HD)], wo_recv)
        project(p)

    for b in range(nz):
        remote(
            down_hbm.at[0, :, blk(2 * b + 1 - core, cw)],
            wd.at[b, blk(core, hw)],
            wd_send,
            wd_recv,
            ctx=pair,
        ).start()
    slot = lax.broadcasted_iota(jnp.int32, (slots, rows), 0)
    wanted = (slot // SLOTS) * nz + z
    hit = jnp.zeros((slots, rows), F32)
    weight = jnp.zeros((slots, rows), F32)
    for copy in small[1:]:
        copy.wait()
    ids, gates = ids_ref[...], gates_ref[...]
    for t in range(ids.shape[0]):
        same = ids[t : t + 1, :] == wanted
        hit = jnp.where(same, 1.0, hit)
        weight = jnp.where(same, gates[t : t + 1, :], weight)
    earlier = lax.broadcasted_iota(jnp.int32, (rows, rows), 0) < lax.broadcasted_iota(
        jnp.int32, (rows, rows), 1
    )
    rank = dot(hit.astype(BF16), earlier.astype(F32).astype(BF16))
    placed = jnp.where(rank == (slot % SLOTS).astype(F32), hit, 0.0)
    place[...] = placed.astype(BF16)
    combine[...] = (placed * weight).T.astype(BF16)
    squares[...] = jnp.zeros_like(squares)
    acc[...] = jnp.zeros_like(acc)

    for p in range(PARTS):
        finish_stream(p)
    blocks[z] = stream[...]

    def dispatch(t):
        b = nearest(t, z, nz)

        @pl.when(t > 0)
        def _():
            for p in range(PARTS):
                wait_for(blocks.at[b, pl.ds(p * pr, pr)], g_recv.at[p, b])

        if nz == 8:

            @pl.when(t == 3)
            def _():
                hand_on(b, nz - 1, nz - 2)

            @pl.when(t == 4)
            def _():
                hand_on(b, 1, 2)

        d_out[b] = dot(place[...], blocks[b]).astype(BF16)
        for peer in peers:
            remote(
                d_out.at[b, blk(peer, SLOTS)],
                d_in.at[b, blk(e, SLOTS), mine],
                d_send.at[b],
                d_recv.at[b],
                exp=peer,
            ).start()
        d_in[b, blk(e, SLOTS), mine] = d_out[b, blk(e, SLOTS)]

    got = pl.ds(0, slots - SLOTS)

    def take(t):
        b = nearest(t, z, nz)
        wait_for(d_in.at[b, got, mine], d_recv.at[b])
        remote(
            d_in.at[b, :, mine], d_in.at[b, :, mine], p_send.at[b], p_recv.at[b], ctx=pair
        ).start()

    def feed(t):
        b = nearest(t, z, nz)
        wait_for(d_in.at[b, :, mine], p_recv.at[b])
        wide = d_in[b].astype(F32)
        squared = wide * wide
        part = squares[...]
        for n in range(2 * cw // 128):
            part = part + squared[:, n * 128 : (n + 1) * 128]
        squares[...] = part
        scaled = (wide * gain_ref[:, blk(b, 2 * cw)]).astype(BF16)
        acc[...] = acc[...] + dot(scaled, w_in[blk(b, 2 * cw), :])

    lag = nz // 2

    def lead(t, carry):
        dispatch(t)
        return carry

    lax.fori_loop(0, lag, lead, 0)
    for half in range(2):
        pltpu.make_async_copy(
            in_hbm.at[half, 0], w_in.at[:, pl.ds(half * hw, hw)], in_load.at[half]
        ).wait()

    def turn_in(t, carry):
        @pl.when(t < nz)
        def _():
            dispatch(t)

        @pl.when(t < nz + lag)
        def _():
            take(t - lag)

        @pl.when(t > lag)
        def _():
            feed(t - lag - 1)

        return carry

    lax.fori_loop(lag, nz + lag + 1, turn_in, 0)

    mean = jnp.sum(squares[...], axis=1, keepdims=True) * (1.0 / (2 * nz * cw))
    inverse = lax.rsqrt(mean + 1e-6)
    gate = acc[:, pl.ds(0, hw)] * inverse
    up = acc[:, pl.ds(hw, hw)] * inverse
    act_mine = act.at[:, blk(core, hw)]
    act[:, blk(core, hw)] = (gate / (1.0 + jnp.exp(-gate)) * up).astype(BF16)
    remote(act_mine, act_mine, act_send, act_recv, ctx=pair).start()
    wait_for(wd.at[:, blk(core, hw)], wd_load)
    wait_for(wd.at[:, blk(core, hw)], wd_recv)
    wait_for(act_mine, act_recv)

    def give(t):
        b = nearest(nz - 1 - t, z, nz)
        r_out[b] = dot(act[...], wd[b]).astype(BF16)
        for peer in peers:
            remote(
                r_out.at[b, blk(peer, SLOTS)],
                r_in.at[b, blk(e, SLOTS)],
                r_send.at[b],
                r_recv.at[b],
                exp=peer,
            ).start()
        r_in[b, blk(e, SLOTS)] = r_out[b, blk(e, SLOTS)]

    def join(t):
        b = nearest(nz - 1 - t, z, nz)
        wait_for(r_in.at[b, got], r_recv.at[b])
        f_out[b] = dot(combine[...], r_in[b]).astype(BF16)

        @pl.when(b != z)
        def _():
            remote(
                f_out.at[b], f_in.at[z], f_send.at[b], f_recv.at[z], ctx=2 * b + core
            ).start()

    def lead_back(t, carry):
        give(t)
        return carry

    lax.fori_loop(0, lag, lead_back, 0)

    def turn_back(t, carry):
        @pl.when(t < nz)
        def _():
            give(t)

        join(t - lag)
        return carry

    lax.fori_loop(lag, nz + lag, turn_back, 0)

    wait_for(wo.at[:, blk(core, 2 * HD)], wo_send)
    wait_for(wd.at[:, blk(core, hw)], wd_send)
    wait_for(act_mine, act_send)

    for p in range(PARTS):
        for half in range(2):
            wait_for(piece(kv, p, half), kv_send.at[p, half])
    wait_for(block_mine, block_send)

    def drain_block(b, carry):
        wait_for(d_out.at[b, got], d_send.at[b])
        wait_for(r_out.at[b, got], r_send.at[b])
        wait_for(d_in.at[b, :, mine], p_send.at[b])
        return carry

    lax.fori_loop(0, nz, drain_block, 0)

    def drain_z(t, carry):
        there = (z + t) % nz
        for p in range(PARTS):
            here = pl.ds(p * pr, pr)
            wait_for(z_out.at[p, there], z_send.at[p, there])
            wait_for(zs_out.at[p, there], zs_send.at[p, there])
            wait_for(c_out.at[p, there], c_send.at[p, there])
        return carry

    lax.fori_loop(1, nz, drain_z, 0)
    for p in range(PARTS):
        here = pl.ds(p * pr, pr)
        for t in range(1, min(nz, 5)):
            there = nearest(t, z, nz)
            wait_for(stream.at[here], g_send.at[p, there])
        if nz == 8:
            for t in (1, nz - 1, 2 if p == 1 else nz - 2):
                wait_for(stream.at[here], h_send.at[p, (z + t) % nz])
    for p in range(PARTS):
        wait_for(att.at[pl.ds(p * pr, pr), mine], att_send.at[p])

    total = f_out[z].astype(F32)
    for t in range(1, nz):
        source = nearest(t, z, nz)
        wait_for(f_in.at[source], f_recv.at[source])
        total = total + f_in[source].astype(F32)
    out_ref[...] = (stream[...].astype(F32) + total).astype(BF16)

    for t in range(1, nz):
        there = nearest(t, z, nz)
        wait_for(f_out.at[there], f_send.at[there])


def body(
    queries,
    cache_kv,
    block_kv,
    stream_in,
    out_proj,
    norm_gain,
    expert_ids,
    gate_weights,
    expert_in,
    expert_out,
):
    ctx_size, ne = lax.axis_size("ctx"), lax.axis_size("exp")
    nz = ctx_size // 2
    rows, width = queries.shape
    seqs = cache_kv.shape[1]
    masked = rows // seqs
    ng = cache_kv.shape[3] // HD
    group = width // HD // ng
    cw, hw = width // ctx_size, expert_in.shape[3]
    slots = ne * SLOTS
    grid = (4, 4) if ne == 16 else (1, ne)
    steps, pr = PARTS * ng, rows // PARTS
    dma, vm = pltpu.SemaphoreType.DMA, pltpu.VMEM
    anyspace = pl.BlockSpec(memory_space=pl.ANY)
    vmem = pl.BlockSpec(memory_space=pltpu.VMEM)
    dims = (nz, ng, ne, grid, seqs, masked, group, cw, hw)
    buffers = [
        vm((rows, width), BF16),
        vm(cache_kv.shape, BF16),
        vm(cache_kv.shape, BF16),
        vm(block_kv.shape, BF16),
        vm((1, width), F32),
        vm(expert_ids.shape[::-1], jnp.int32),
        vm(gate_weights.shape[::-1], F32),
        vm((2, seqs, 128, cache_kv.shape[3]), BF16),
        vm((rows, cw), BF16),
        vm((nz, 4 * HD, cw), BF16),
        vm((width, 2 * hw), BF16),
        vm((nz, 2 * hw, cw), BF16),
        vm((128, 128), F32),
        vm((PARTS, nz, pr, 2 * HD), BF16),
        vm((PARTS, nz, pr, 2 * HD), BF16),
        vm((PARTS, nz, 8, 128), F32),
        vm((PARTS, nz, 8, 128), F32),
        vm((rows, 4 * HD), BF16),
        vm((PARTS, nz, pr, cw), BF16),
        vm((PARTS, nz, pr, cw), BF16),
        vm((rows, cw), BF16),
        vm((nz, rows, cw), BF16),
        vm((slots, rows), BF16),
        vm((rows, slots), BF16),
        vm((nz, slots, cw), BF16),
        vm((nz, slots, 2 * cw), BF16),
        vm((slots, 128), F32),
        vm((slots, 2 * hw), F32),
        vm((slots, 2 * hw), BF16),
        vm((nz, slots, cw), BF16),
        vm((nz, slots, cw), BF16),
        vm((nz, rows, cw), BF16),
        vm((nz, rows, cw), BF16),
    ]
    counts = [(4,), (PARTS,), (PARTS, 2)] + [()] * 4 + [(2,)] + [()] * 3
    counts += [(PARTS, 2)] * 2 + [()] * 2 + [(PARTS, nz)] * 4 + [(PARTS,)] * 2 + [(PARTS, nz)] * 5
    counts += [(nz,)] * 4 + [()] * 2 + [(nz,)] * 4
    return pl.pallas_call(
        functools.partial(layer_kernel, dims),
        out_shape=jax.ShapeDtypeStruct((rows, cw), BF16),
        in_specs=[anyspace] * 10,
        out_specs=vmem,
        scratch_shapes=buffers + [dma(shape) for shape in counts],
        compiler_params=pltpu.CompilerParams(
            collective_id=1, has_side_effects=True, vmem_limit_bytes=VMEM_LIMIT
        ),
    )(
        queries,
        cache_kv,
        block_kv,
        stream_in,
        out_proj,
        norm_gain.reshape(1, width),
        expert_ids.T,
        gate_weights.T,
        expert_in,
        expert_out,
    )


def solution(mesh):
    placed = (
        P("exp", None),
        P(None, "exp", "ctx", None),
        P(None, "exp", "ctx", None),
        P("exp", None),
        P("ctx", None),
        P(),
        P("exp", None),
        P("exp", None),
        P(None, "exp", None, "ctx"),
        P("exp", "ctx", None),
    )
    return jax.shard_map(
        body, mesh=mesh, in_specs=placed, out_specs=P("exp", "ctx"), check_vma=False
    )
```

```python
import functools
import math

import jax
import jax.numpy as jnp
from jax import lax
from jax.experimental import pallas as pl
from jax.experimental.pallas import tpu as pltpu
from jax.sharding import PartitionSpec as P

HD = 128
SLOTS = 16
PARTS = 2
MESH = pl.DeviceIdType.MESH
F32 = jnp.float32
BF16 = jnp.bfloat16
VMEM_LIMIT = 60 * 1024 * 1024


def dot(a, b):
    return jnp.dot(a, b, preferred_element_type=F32)


def dot_t(a, b):
    return lax.dot_general(a, b, (((1,), (1,)), ((), ())), preferred_element_type=F32)


def remote(src, dst, send_sem, recv_sem, **where):
    return pltpu.make_async_remote_copy(
        src_ref=src,
        dst_ref=dst,
        send_sem=send_sem,
        recv_sem=recv_sem,
        device_id=where,
        device_id_type=MESH,
    )


def wait_for(ref, sem):
    pltpu.make_async_copy(ref, ref, sem).wait()


def blk(index, size):
    return pl.ds(pl.multiple_of(index * size, size), size)


def nearest(step, here, count):
    odd = step % 2
    return (here + odd * ((step + 1) // 2) + (1 - odd) * (count - step // 2)) % count


def layer_kernel(
    dims,
    q_hbm,
    cache_hbm,
    block_hbm,
    stream_hbm,
    proj_hbm,
    gain_hbm,
    ids_hbm,
    gates_hbm,
    in_hbm,
    down_hbm,
    out_ref,
    q,
    kv,
    kv_pair,
    block_ref,
    gain_ref,
    ids_ref,
    gates_ref,
    block,
    sin,
    wo,
    w_in,
    wd,
    stat,
    z_out,
    z_in,
    zs_out,
    zs_in,
    att,
    c_out,
    c_in,
    stream,
    blocks,
    place,
    combine,
    d_out,
    d_in,
    squares,
    acc,
    act,
    r_out,
    r_in,
    f_out,
    f_in,
    small_load,
    q_load,
    kv_load,
    sin_load,
    wo_load,
    wo_send,
    wo_recv,
    in_load,
    wd_load,
    wd_send,
    wd_recv,
    kv_send,
    kv_recv,
    block_send,
    block_recv,
    z_send,
    z_recv,
    zs_send,
    zs_recv,
    att_send,
    att_recv,
    c_send,
    c_recv,
    g_send,
    g_recv,
    h_send,
    d_send,
    d_recv,
    p_send,
    p_recv,
    act_send,
    act_recv,
    r_send,
    r_recv,
    f_send,
    f_recv,
):
    nz, ng, ne, grid, seqs, masked, group, cw, hw = dims
    ctx, e = lax.axis_index("ctx"), lax.axis_index("exp")
    z, core = ctx // 2, ctx % 2
    pair = 2 * z + 1 - core
    rows = seqs * masked
    span = seqs // PARTS
    pr = rows // PARTS
    steps = PARTS * ng
    slots = ne * SLOTS
    mine = blk(core, cw)
    factor = HD**-0.5 * math.log2(math.e)
    ny = grid[1]
    ex, ey = e // ny, e % ny
    peers = []
    steps_away = [min(t // ny, grid[0] - t // ny) + min(t % ny, ny - t % ny) for t in range(ne)]
    for t in sorted(range(1, ne), key=lambda t: -steps_away[t]):
        peers.append(((ex + t // ny) % grid[0]) * ny + (ey + t % ny) % ny)

    def place_of(k):
        return k // ng, (z // 2 + ng // 2 + k % ng) % ng

    def piece(ref, p, half):
        return ref.at[half, blk(p, span)]

    def part_load(p):
        copies = [pltpu.make_async_copy(q_hbm.at[blk(p, pr)], q.at[blk(p, pr)], q_load.at[p])]
        for half in range(2):
            copies.append(
                pltpu.make_async_copy(
                    piece(cache_hbm, p, half), piece(kv, p, half), kv_load.at[p, half]
                )
            )
        return copies

    barrier = pltpu.get_barrier_semaphore()
    pl.semaphore_signal(barrier, inc=1, device_id={"ctx": pair}, device_id_type=MESH)
    for copy in part_load(0):
        copy.start()
    for t in range(1, nz):
        there = 2 * ((z + t) % nz) + core
        pl.semaphore_signal(barrier, inc=1, device_id={"ctx": there}, device_id_type=MESH)
    for peer in peers:
        pl.semaphore_signal(barrier, inc=1, device_id={"exp": peer}, device_id_type=MESH)

    for p in range(1, PARTS):
        for copy in part_load(p):
            copy.start()
    small = [
        pltpu.make_async_copy(source, here, small_load.at[n])
        for n, (source, here) in enumerate(
            [
                (block_hbm, block_ref),
                (gain_hbm, gain_ref),
                (ids_hbm, ids_ref),
                (gates_hbm, gates_ref),
            ]
        )
    ]
    for copy in small:
        copy.start()

    pl.semaphore_wait(barrier, nz + ne - 1)

    for p in range(PARTS):
        for half in range(2):
            remote(
                piece(cache_hbm, p, half),
                piece(kv_pair, p, half),
                kv_send.at[p, half],
                kv_recv.at[p, half],
                ctx=pair,
            ).start()
    block_rows = block_ref.shape[2]
    small[0].wait()
    block[:, :, pl.ds(0, 16)] = jnp.zeros((2, seqs, 16, block.shape[3]), BF16)
    block[:, :, pl.ds(32, 96)] = jnp.zeros((2, seqs, 96, block.shape[3]), BF16)
    for s in range(seqs):
        for half in range(2):
            block[half, s, pl.ds(0, block_rows), :] = block_ref[half, s]

    block_mine = block.at[:, :, pl.ds(0, 16)]
    remote(
        block_mine, block.at[:, :, pl.ds(16, 16)], block_send, block_recv, ctx=pair
    ).start()

    load_sin = pltpu.make_async_copy(stream_hbm.at[:, blk(ctx, cw)], sin, sin_load)
    load_sin.start()
    for b in range(nz):
        pltpu.make_async_copy(
            proj_hbm.at[:, blk(2 * b + core, cw)], wo.at[b, blk(core, 2 * HD)], wo_load
        ).start()
    for b in range(nz):
        remote(
            proj_hbm.at[:, blk(2 * b + 1 - core, cw)],
            wo.at[b, blk(core, 2 * HD)],
            wo_send,
            wo_recv,
            ctx=pair,
        ).start()

    lane = lax.broadcasted_iota(jnp.int32, (masked, 128), 1)
    block_lane = lax.broadcasted_iota(jnp.int32, (group // 2 * masked, 128), 1)
    block_live = (block_lane < 32) & (block_lane % 16 < block_rows)
    ones_keys = jnp.ones((kv.shape[2], HD), BF16)
    ones_block = jnp.ones((128, HD), BF16)

    def await_keys(p):
        for copy in part_load(p)[:2]:
            copy.wait()

    def await_pair_keys(p):
        wait_for(piece(kv_pair, p, 0), kv_recv.at[p, 0])

    def await_values(p):
        part_load(p)[2].wait()
        wait_for(piece(kv_pair, p, 1), kv_recv.at[p, 1])

    def attend(k, first):
        p, j = place_of(k)
        if first:
            await_keys(0)
        else:

            @pl.when(k % ng == 0)
            def _():
                await_keys(p)
                await_pair_keys(p)
                await_values(p)

        column = blk(j, HD)
        heads = [j * group + (m // 2) * 4 + 2 * core + m % 2 for m in range(4)]
        which = [p * span + n for n in range(span)]
        asked = [
            jnp.concatenate([q[blk(s, masked), blk(h, HD)] for h in heads], axis=0) for s in which
        ]
        own_scores = [dot_t(qs, kv[0, s, :, column]) for qs, s in zip(asked, which)]
        if first:
            wait_for(block_mine, block_recv)
            await_pair_keys(0)
        scores = []
        for qs, s, own in zip(asked, which, own_scores):
            extra = jnp.where(block_live, dot_t(qs, block[0, s, :, column]), -1e30)
            scores.append([own, dot_t(qs, kv_pair[0, s, :, column]), extra])
        peaks = []
        for own, other, extra in scores:
            widest = extra
            for m in range(kv.shape[2] // 128):
                cut = slice(m * 128, (m + 1) * 128)
                widest = jnp.maximum(widest, jnp.maximum(own[:, cut], other[:, cut]))
            peaks.append(jnp.max(widest, axis=1, keepdims=True))
        weights = [
            [jnp.exp2((part - peak) * factor).astype(BF16) for part in parts]
            for parts, peak in zip(scores, peaks)
        ]
        if first:
            await_values(0)
        for n, s in enumerate(which):
            local = pl.ds(n * masked, masked)
            both = dot(weights[n][0], jnp.concatenate([kv[1, s, :, column], ones_keys], axis=1))
            both += dot(
                weights[n][1], jnp.concatenate([kv_pair[1, s, :, column], ones_keys], axis=1)
            )
            both += dot(
                weights[n][2], jnp.concatenate([block[1, s, :, column], ones_block], axis=1)
            )
            summed, total = both[:, :HD].astype(BF16), both[:, HD:]
            peak = peaks[n] * factor
            stats = jnp.zeros((masked, 128), F32)
            for m in range(4):
                zz, h = m // 2, m % 2
                cut = slice(m * masked, (m + 1) * masked)
                stats = jnp.where(lane == zz * 8 + h, peak[cut], stats)
                stats = jnp.where(lane == zz * 8 + h + 2, total[cut], stats)
                z_out[p, 2 * j + zz, local, pl.ds(h * HD, HD)] = summed[cut]
            stat[local, :] = stats
        turned = stat[...].T
        for zz in range(2):
            there = 2 * j + zz
            zs_out[p, there] = turned[zz * 8 : zz * 8 + 8]

            @pl.when(there == z)
            def _():
                z_in[p, there] = z_out[p, there]
                zs_in[p, there] = zs_out[p, there]

            @pl.when(there != z)
            def _():
                remote(
                    z_out.at[p, there],
                    z_in.at[p, z],
                    z_send.at[p, there],
                    z_recv.at[p, z],
                    ctx=2 * there + core,
                ).start()
                remote(
                    zs_out.at[p, there],
                    zs_in.at[p, z],
                    zs_send.at[p, there],
                    zs_recv.at[p, z],
                    ctx=2 * there + core,
                ).start()

    stat[...] = jnp.zeros_like(stat)
    attend(0, True)

    def turn(k, carry):
        attend(k, False)
        return carry

    lax.fori_loop(1, steps, turn, 0)
    for half in range(2):
        pltpu.make_async_copy(
            in_hbm.at[half, 0], w_in.at[:, pl.ds(half * hw, hw)], in_load.at[half]
        ).start()
    for b in range(nz):
        pltpu.make_async_copy(
            down_hbm.at[0, :, blk(2 * b + core, cw)], wd.at[b, blk(core, hw)], wd_load
        ).start()


    def finish_heads(p):
        for t in range(1, nz):
            source = (z + t) % nz
            wait_for(z_in.at[p, source], z_recv.at[p, source])
            wait_for(zs_in.at[p, source], zs_recv.at[p, source])
        here = pl.ds(p * pr, pr)
        peaks = [zs_in[p, b, pl.ds(0, 2), :] for b in range(nz)]
        peak = functools.reduce(jnp.maximum, peaks)
        factors = [jnp.exp2(one - peak) for one in peaks]
        total = jnp.zeros((2, 128), F32)
        for b in range(nz):
            total = total + zs_in[p, b, pl.ds(2, 2), :] * factors[b]
        for b in range(nz):
            zs_in[p, b, pl.ds(4, 2), :] = factors[b] / total
        turned = jnp.concatenate([zs_in[p, b] for b in range(nz)], axis=0).T
        for h in range(2):
            summed = jnp.zeros((pr, HD), F32)
            for b in range(nz):
                f = turned[:pr, 8 * b + h + 4 : 8 * b + h + 5]
                summed = summed + z_in[p, b, :, pl.ds(h * HD, HD)].astype(F32) * f
            att[here, blk(2 * core + h, HD)] = summed.astype(BF16)
        return remote(
            att.at[here, mine], att.at[here, mine], att_send.at[p], att_recv.at[p], ctx=pair
        )

    def project(p):
        here = pl.ds(p * pr, pr)
        wait_for(att.at[here, mine], att_recv.at[p])
        heads = att[here, :]
        for t in range(1, nz):
            there = nearest(nz - t, z, nz)
            c_out[p, there] = dot(heads, wo[there]).astype(BF16)
            remote(
                c_out.at[p, there],
                c_in.at[p, z],
                c_send.at[p, there],
                c_recv.at[p, z],
                ctx=2 * there + core,
            ).start()

    def finish_stream(p):
        here = pl.ds(p * pr, pr)
        total = dot(att[here, :], wo[z]) + sin[here, :].astype(F32)
        for t in range(1, nz):
            source = nearest(t, z, nz)
            wait_for(c_in.at[p, source], c_recv.at[p, source])
            total = total + c_in[p, source].astype(F32)
        stream[here, :] = total.astype(BF16)
        for t in range(1, min(nz, 5)):
            there = nearest(t, z, nz)
            remote(
                stream.at[here],
                blocks.at[z, here],
                g_send.at[p, there],
                g_recv.at[p, z],
                ctx=2 * there + core,
            ).start()

    def hand_on(b, first, second):
        for p in range(PARTS):
            here = pl.ds(p * pr, pr)
            there = (z + first) % nz
            remote(
                blocks.at[b, here],
                blocks.at[b, here],
                h_send.at[p, there],
                g_recv.at[p, b],
                ctx=2 * there + core,
            ).start()
        here = pl.ds((first == 1) * pr, pr)
        there = (z + second) % nz
        part = int(first == 1)
        remote(
            blocks.at[b, here],
            blocks.at[b, here],
            h_send.at[part, there],
            g_recv.at[part, b],
            ctx=2 * there + core,
        ).start()

    load_sin.wait()
    wait_for(wo.at[:, blk(core, 2 * HD)], wo_load)
    for p in range(PARTS):
        finish_heads(p).start()
        if p == 0:
            wait_for(wo.at[:, blk(core, 2 * HD)], wo_recv)
        project(p)

    for b in range(nz):
        remote(
            down_hbm.at[0, :, blk(2 * b + 1 - core, cw)],
            wd.at[b, blk(core, hw)],
            wd_send,
            wd_recv,
            ctx=pair,
        ).start()
    slot = lax.broadcasted_iota(jnp.int32, (slots, rows), 0)
    wanted = (slot // SLOTS) * nz + z
    hit = jnp.zeros((slots, rows), F32)
    weight = jnp.zeros((slots, rows), F32)
    for copy in small[1:]:
        copy.wait()
    ids, gates = ids_ref[...], gates_ref[...]
    for t in range(ids.shape[0]):
        same = ids[t : t + 1, :] == wanted
        hit = jnp.where(same, 1.0, hit)
        weight = jnp.where(same, gates[t : t + 1, :], weight)
    earlier = lax.broadcasted_iota(jnp.int32, (rows, rows), 0) < lax.broadcasted_iota(
        jnp.int32, (rows, rows), 1
    )
    rank = dot(hit.astype(BF16), earlier.astype(F32).astype(BF16))
    placed = jnp.where(rank == (slot % SLOTS).astype(F32), hit, 0.0)
    place[...] = placed.astype(BF16)
    combine[...] = (placed * weight).T.astype(BF16)
    squares[...] = jnp.zeros_like(squares)
    acc[...] = jnp.zeros_like(acc)

    for p in range(PARTS):
        finish_stream(p)
    blocks[z] = stream[...]

    def dispatch(t):
        b = nearest(t, z, nz)

        @pl.when(t > 0)
        def _():
            for p in range(PARTS):
                wait_for(blocks.at[b, pl.ds(p * pr, pr)], g_recv.at[p, b])

        if nz == 8:

            @pl.when(t == 3)
            def _():
                hand_on(b, nz - 1, nz - 2)

            @pl.when(t == 4)
            def _():
                hand_on(b, 1, 2)

        d_out[b] = dot(place[...], blocks[b]).astype(BF16)
        for peer in peers:
            remote(
                d_out.at[b, blk(peer, SLOTS)],
                d_in.at[b, blk(e, SLOTS), mine],
                d_send.at[b],
                d_recv.at[b],
                exp=peer,
            ).start()
        d_in[b, blk(e, SLOTS), mine] = d_out[b, blk(e, SLOTS)]

    got = pl.ds(0, slots - SLOTS)

    def take(t):
        b = nearest(t, z, nz)
        wait_for(d_in.at[b, got, mine], d_recv.at[b])
        remote(
            d_in.at[b, :, mine], d_in.at[b, :, mine], p_send.at[b], p_recv.at[b], ctx=pair
        ).start()

    def feed(t):
        b = nearest(t, z, nz)
        wait_for(d_in.at[b, :, mine], p_recv.at[b])
        wide = d_in[b].astype(F32)
        squared = wide * wide
        part = squares[...]
        for n in range(2 * cw // 128):
            part = part + squared[:, n * 128 : (n + 1) * 128]
        squares[...] = part
        scaled = (wide * gain_ref[:, blk(b, 2 * cw)]).astype(BF16)
        acc[...] = acc[...] + dot(scaled, w_in[blk(b, 2 * cw), :])

    lag = nz // 2

    def lead(t, carry):
        dispatch(t)
        return carry

    lax.fori_loop(0, lag, lead, 0)
    for half in range(2):
        pltpu.make_async_copy(
            in_hbm.at[half, 0], w_in.at[:, pl.ds(half * hw, hw)], in_load.at[half]
        ).wait()

    def turn_in(t, carry):
        @pl.when(t < nz)
        def _():
            dispatch(t)

        @pl.when(t < nz + lag)
        def _():
            take(t - lag)

        @pl.when(t > lag)
        def _():
            feed(t - lag - 1)

        return carry

    lax.fori_loop(lag, nz + lag + 1, turn_in, 0)

    mean = jnp.sum(squares[...], axis=1, keepdims=True) * (1.0 / (2 * nz * cw))
    inverse = lax.rsqrt(mean + 1e-6)
    gate = acc[:, pl.ds(0, hw)] * inverse
    up = acc[:, pl.ds(hw, hw)] * inverse
    act_mine = act.at[:, blk(core, hw)]
    act[:, blk(core, hw)] = (gate / (1.0 + jnp.exp(-gate)) * up).astype(BF16)
    remote(act_mine, act_mine, act_send, act_recv, ctx=pair).start()
    wait_for(wd.at[:, blk(core, hw)], wd_load)
    wait_for(wd.at[:, blk(core, hw)], wd_recv)
    wait_for(act_mine, act_recv)

    def give(t):
        b = nearest(nz - 1 - t, z, nz)
        r_out[b] = dot(act[...], wd[b]).astype(BF16)
        for peer in peers:
            remote(
                r_out.at[b, blk(peer, SLOTS)],
                r_in.at[b, blk(e, SLOTS)],
                r_send.at[b],
                r_recv.at[b],
                exp=peer,
            ).start()
        r_in[b, blk(e, SLOTS)] = r_out[b, blk(e, SLOTS)]

    def join(t):
        b = nearest(nz - 1 - t, z, nz)
        wait_for(r_in.at[b, got], r_recv.at[b])
        f_out[b] = dot(combine[...], r_in[b]).astype(BF16)

        @pl.when(b != z)
        def _():
            remote(
                f_out.at[b], f_in.at[z], f_send.at[b], f_recv.at[z], ctx=2 * b + core
            ).start()

    def lead_back(t, carry):
        give(t)
        return carry

    lax.fori_loop(0, lag, lead_back, 0)

    def turn_back(t, carry):
        @pl.when(t < nz)
        def _():
            give(t)

        join(t - lag)
        return carry

    lax.fori_loop(lag, nz + lag, turn_back, 0)

    wait_for(wo.at[:, blk(core, 2 * HD)], wo_send)
    wait_for(wd.at[:, blk(core, hw)], wd_send)
    wait_for(act_mine, act_send)

    for p in range(PARTS):
        for half in range(2):
            wait_for(piece(kv, p, half), kv_send.at[p, half])
    wait_for(block_mine, block_send)

    def drain_block(b, carry):
        wait_for(d_out.at[b, got], d_send.at[b])
        wait_for(r_out.at[b, got], r_send.at[b])
        wait_for(d_in.at[b, :, mine], p_send.at[b])
        return carry

    lax.fori_loop(0, nz, drain_block, 0)

    def drain_z(t, carry):
        there = (z + t) % nz
        for p in range(PARTS):
            here = pl.ds(p * pr, pr)
            wait_for(z_out.at[p, there], z_send.at[p, there])
            wait_for(zs_out.at[p, there], zs_send.at[p, there])
            wait_for(c_out.at[p, there], c_send.at[p, there])
        return carry

    lax.fori_loop(1, nz, drain_z, 0)
    for p in range(PARTS):
        here = pl.ds(p * pr, pr)
        for t in range(1, min(nz, 5)):
            there = nearest(t, z, nz)
            wait_for(stream.at[here], g_send.at[p, there])
        if nz == 8:
            for t in (1, nz - 1, 2 if p == 1 else nz - 2):
                wait_for(stream.at[here], h_send.at[p, (z + t) % nz])
    for p in range(PARTS):
        wait_for(att.at[pl.ds(p * pr, pr), mine], att_send.at[p])

    total = f_out[z].astype(F32)
    for t in range(1, nz):
        source = nearest(t, z, nz)
        wait_for(f_in.at[source], f_recv.at[source])
        total = total + f_in[source].astype(F32)
    out_ref[...] = (stream[...].astype(F32) + total).astype(BF16)

    for t in range(1, nz):
        there = nearest(t, z, nz)
        wait_for(f_out.at[there], f_send.at[there])


def body(
    queries,
    cache_kv,
    block_kv,
    stream_in,
    out_proj,
    norm_gain,
    expert_ids,
    gate_weights,
    expert_in,
    expert_out,
):
    ctx_size, ne = lax.axis_size("ctx"), lax.axis_size("exp")
    nz = ctx_size // 2
    rows, width = queries.shape
    seqs = cache_kv.shape[1]
    masked = rows // seqs
    ng = cache_kv.shape[3] // HD
    group = width // HD // ng
    cw, hw = width // ctx_size, expert_in.shape[3]
    slots = ne * SLOTS
    grid = (4, 4) if ne == 16 else (1, ne)
    steps, pr = PARTS * ng, rows // PARTS
    dma, vm = pltpu.SemaphoreType.DMA, pltpu.VMEM
    anyspace = pl.BlockSpec(memory_space=pl.ANY)
    vmem = pl.BlockSpec(memory_space=pltpu.VMEM)
    dims = (nz, ng, ne, grid, seqs, masked, group, cw, hw)
    buffers = [
        vm((rows, width), BF16),
        vm(cache_kv.shape, BF16),
        vm(cache_kv.shape, BF16),
        vm(block_kv.shape, BF16),
        vm((1, width), F32),
        vm(expert_ids.shape[::-1], jnp.int32),
        vm(gate_weights.shape[::-1], F32),
        vm((2, seqs, 128, cache_kv.shape[3]), BF16),
        vm((rows, cw), BF16),
        vm((nz, 4 * HD, cw), BF16),
        vm((width, 2 * hw), BF16),
        vm((nz, 2 * hw, cw), BF16),
        vm((128, 128), F32),
        vm((PARTS, nz, pr, 2 * HD), BF16),
        vm((PARTS, nz, pr, 2 * HD), BF16),
        vm((PARTS, nz, 8, 128), F32),
        vm((PARTS, nz, 8, 128), F32),
        vm((rows, 4 * HD), BF16),
        vm((PARTS, nz, pr, cw), BF16),
        vm((PARTS, nz, pr, cw), BF16),
        vm((rows, cw), BF16),
        vm((nz, rows, cw), BF16),
        vm((slots, rows), BF16),
        vm((rows, slots), BF16),
        vm((nz, slots, cw), BF16),
        vm((nz, slots, 2 * cw), BF16),
        vm((slots, 128), F32),
        vm((slots, 2 * hw), F32),
        vm((slots, 2 * hw), BF16),
        vm((nz, slots, cw), BF16),
        vm((nz, slots, cw), BF16),
        vm((nz, rows, cw), BF16),
        vm((nz, rows, cw), BF16),
    ]
    counts = [(4,), (PARTS,), (PARTS, 2)] + [()] * 4 + [(2,)] + [()] * 3
    counts += [(PARTS, 2)] * 2 + [()] * 2 + [(PARTS, nz)] * 4 + [(PARTS,)] * 2 + [(PARTS, nz)] * 5
    counts += [(nz,)] * 4 + [()] * 2 + [(nz,)] * 4
    return pl.pallas_call(
        functools.partial(layer_kernel, dims),
        out_shape=jax.ShapeDtypeStruct((rows, cw), BF16),
        in_specs=[anyspace] * 10,
        out_specs=vmem,
        scratch_shapes=buffers + [dma(shape) for shape in counts],
        compiler_params=pltpu.CompilerParams(
            collective_id=1, has_side_effects=True, vmem_limit_bytes=VMEM_LIMIT
        ),
    )(
        queries,
        cache_kv,
        block_kv,
        stream_in,
        out_proj,
        norm_gain.reshape(1, width),
        expert_ids.T,
        gate_weights.T,
        expert_in,
        expert_out,
    )


def solution(mesh):
    placed = (
        P("exp", None),
        P(None, "exp", "ctx", None),
        P(None, "exp", "ctx", None),
        P("exp", None),
        P("ctx", None),
        P(),
        P("exp", None),
        P("exp", None),
        P(None, "exp", None, "ctx"),
        P("exp", "ctx", None),
    )
    return jax.shard_map(
        body, mesh=mesh, in_specs=placed, out_specs=P("exp", "ctx"), check_vma=False
    )
```
